32 devices in a mesh: dp: 4 (over y, x), ctx: 8 (over z, core).
Axes of the slice: x: 2, y: 2, z: 4, core: 2. Of those that a mesh axis runs over, the one named last changes fastest.
Arguments:
- inputs: bfloat16 [4, 64, 8192], P('dp', None, 'ctx'), may hold values from -6 to 6
- cotangent: bfloat16 [4, 64, 8192], P('dp', None, 'ctx'), may hold values from -6 to 6
- filters: float32 [64, 8192], P(None, 'ctx'), may hold values from -6 to 6
- skip_gain: float32 [64], replicated, may hold values from 0.1 to 1.9
Outputs:
- input_grad: bfloat16 [4, 64, 8192], P('dp', None, 'ctx')
- filter_grad: float32 [64, 8192], P(None, 'ctx')
The draws below stay inside these ranges and needn't reach their ends.
All inputs are finite; a program needn't handle non-finite values.
Results may differ from the reference program's by a relative error of at most 0.001.
Values sent between devices are 32-bit elements; how exact they have to be, the bound alone decides.
A program may use at most 128 MiB of HBM per device.

```python
import math
import jax
import jax.numpy as jnp
from jax import lax

C = 64
BATCH = 4
LENGTH = 8192


def level_of(stream_key, dims, split, low, top_value):
    gain = 1.0
    for position, shards_of in split:
        draws = jax.random.uniform(jax.random.fold_in(jax.random.fold_in(stream_key, 6), position), (shards_of,), jnp.float32, low / len(split), top_value / len(split))
        gain = gain * jnp.repeat(jnp.exp(draws), dims[position] // shards_of).reshape((-1,) + (1,) * (len(dims) - 1 - position))
    return gain


def centred(own_key, dims, deviation, most, cuts=(), held_as=jnp.bfloat16):
    factor_of = level_of(own_key, dims, cuts, -0.22, 0.18) if cuts else 1.0
    drawn = jax.random.normal(own_key, dims, jnp.float32) * deviation * factor_of
    return jnp.minimum(jnp.maximum(drawn, -most), most).astype(held_as)


def setup_inputs(seed: int = 0) -> dict:
    arg_keys = jax.random.split(jax.random.key(seed), 5)
    return {
        "inputs": centred(arg_keys[0], (BATCH, C, LENGTH), 1.0, 6.0, ((0, 4), (2, 8))),
        "cotangent": centred(arg_keys[1], (BATCH, C, LENGTH), 1.0, 6.0, ((0, 4), (2, 8))),
        "filters": centred(arg_keys[2], (C, LENGTH), 1.0, 6.0, ((1, 8),), jnp.float32),
        "skip_gain": jnp.clip(1.0 + 0.18 * jax.random.normal(arg_keys[3], (C,), jnp.float32), 0.1, 1.9),
    }


def reference(inputs, cotangent, filters, skip_gain):
    padded_length = 2 * LENGTH
    factor = 1.0 / math.sqrt(LENGTH)
    grad_rows = cotangent.astype(jnp.float32)
    grad_spec = jnp.fft.rfft(grad_rows, n=padded_length, axis=-1)
    input_spec = jnp.fft.rfft(inputs.astype(jnp.float32), n=padded_length, axis=-1)
    filter_spec = jnp.fft.rfft(filters, n=padded_length, axis=-1)
    through = jnp.fft.irfft(jnp.conj(filter_spec)[None] * grad_spec, n=padded_length, axis=-1)[..., :LENGTH]
    input_grad = through * factor + skip_gain[None, :, None] * grad_rows
    summed = lax.optimization_barrier(jnp.sum(jnp.conj(input_spec) * grad_spec, axis=0))
    filter_grad = jnp.fft.irfft(summed, n=padded_length, axis=-1)[:, :LENGTH] * factor
    return (input_grad.astype(jnp.bfloat16), filter_grad.astype(jnp.float32))
```

```python
import functools
import math

import jax
import jax.numpy as jnp
import ml_dtypes
import numpy as np
from jax import lax
from jax.experimental import pallas as pl
from jax.experimental.pallas import tpu as pltpu
from jax.sharding import PartitionSpec as P

LANES = 128
MESH = pl.DeviceIdType.MESH


def dft_tables(length):
    half = length // LANES
    row = np.arange(half)
    lane = np.arange(LANES)
    theta = 2 * math.pi / (2 * half) * (((row[:, None] + 0.5) * row[None, :]) % (2 * half))
    outer = np.concatenate([np.cos(theta), -np.sin(theta)])
    phi = math.pi / length * ((row[:, None] + 0.5) * lane[None, :])
    phi_table = np.stack([np.cos(phi), -np.sin(phi)])
    psi = 2 * math.pi / LANES * ((lane[:, None] * lane[None, :]) % LANES)
    cos, sin = np.cos(psi), np.sin(psi)
    inner = np.block([[cos, -sin], [sin, cos]])
    back = outer.T / length / math.sqrt(length)
    return outer, phi_table.astype(np.float32), inner, back


def np_split(table):
    high = table.astype(ml_dtypes.bfloat16)
    low = (table - high.astype(np.float64)).astype(ml_dtypes.bfloat16)
    return high, low


def split(values):
    high = values.astype(jnp.bfloat16)
    return high, (values - high.astype(jnp.float32)).astype(jnp.bfloat16)


def dot(left, right):
    return jnp.dot(left, right, preferred_element_type=jnp.float32)


def plain_gradients(grads, inputs, filters):
    batch, channels, length = grads.shape
    half = length // LANES
    outer, phi, inner, back = dft_tables(length)
    outer, inner, back = (t.astype(np.float32) for t in (outer, inner, back))
    product = functools.partial(jnp.matmul, precision=lax.Precision.HIGHEST)

    def forward(values):
        rows = product(outer, values.reshape(values.shape[:-1] + (half, LANES)))
        real, imag = rows[..., :half, :], rows[..., half:, :]
        turned = jnp.concatenate(
            [real * phi[0] - imag * phi[1], real * phi[1] + imag * phi[0]], axis=-1
        )
        spec = product(turned, inner)
        return spec[..., :LANES], spec[..., LANES:]

    def backward(real, imag):
        rows = product(jnp.concatenate([real, imag], axis=-1), inner.T)
        real, imag = rows[..., :LANES], rows[..., LANES:]
        turned = jnp.concatenate(
            [real * phi[0] + imag * phi[1], imag * phi[0] - real * phi[1]], axis=-2
        )
        out = product(back, turned)
        return out.reshape(out.shape[:-2] + (length,))

    def conj_product(first, second):
        return (
            first[0] * second[0] + first[1] * second[1],
            first[0] * second[1] - first[1] * second[0],
        )

    grad_spec = forward(grads)
    through = backward(*conj_product(forward(filters), grad_spec))
    real, imag = conj_product(forward(inputs), grad_spec)
    return through, backward(real.sum(0), imag.sum(0))


def plain_body(inputs, cotangent, filters, skip_gain):
    def gather(values):
        return lax.all_to_all(values, "ctx", 0, 1, tiled=True)

    grad_rows = cotangent[0].astype(jnp.float32)
    grads, rows = gather(grad_rows), gather(inputs[0].astype(jnp.float32))
    through, filter_grad = plain_gradients(grads[None], rows[None], gather(filters))
    filter_grad = lax.psum(filter_grad, "dp")
    through = lax.all_to_all(through[0], "ctx", 1, 0, tiled=True)
    filter_grad = lax.all_to_all(filter_grad, "ctx", 1, 0, tiled=True)
    return (through + skip_gain[:, None] * grad_rows).astype(jnp.bfloat16)[None], filter_grad


def kernel(
    groups, parts, count, half,
    x_ref, g_ref, f_ref, outer_ref, outer3_ref, phi_ref, inner_ref, inner_t_ref, back_ref,
    out_ref,
    send_gx, send_f, recv_gx, recv_f, send_out,
    gx_send, gx_recv, f_send, f_recv, out_send, out_recv,
):
    devices = groups * parts
    rows = x_ref.shape[2] // LANES
    group, part = lax.axis_index("dp"), lax.axis_index("ctx")
    me = group * parts + part

    barrier = pltpu.get_barrier_semaphore()

    @pl.loop(1, devices)
    def _(step):
        other = lax.rem(me + step, devices)
        pl.semaphore_signal(
            barrier, inc=1, device_id=(other // parts, lax.rem(other, parts)),
            device_id_type=MESH,
        )

    for i in range(count):
        own = slice(i * devices, (i + 1) * devices)
        for r in range(rows):
            lanes = slice(r * LANES, (r + 1) * LANES)
            send_gx[i, :, 0, r, :] = g_ref[0, own, lanes].astype(jnp.float32)
            send_gx[i, :, 1, r, :] = x_ref[0, own, lanes].astype(jnp.float32)
            send_f[i, :, r, :] = f_ref[own, lanes]

    pl.semaphore_wait(barrier, devices - 1)

    def filter_copy(i, step, to):
        other = lax.rem(part + step, parts) if to else lax.rem(part - step + parts, parts)
        return pltpu.make_async_remote_copy(
            src_ref=send_f.at[i, group * parts + other],
            dst_ref=recv_f.at[i, part if to else other],
            send_sem=f_send.at[i, step],
            recv_sem=f_recv.at[i, step],
            device_id=(group, other),
            device_id_type=MESH,
        )

    def row_copy(i, step, to):
        lead, rest = step // parts, lax.rem(step, parts)
        if to:
            there = (lax.rem(group + lead, groups), lax.rem(part + rest, parts))
            slot = (group, part)
        else:
            there = (lax.rem(group - lead + groups, groups), lax.rem(part - rest + parts, parts))
            slot = there
        return pltpu.make_async_remote_copy(
            src_ref=send_gx.at[i, there[0] * parts + there[1]],
            dst_ref=recv_gx.at[i, slot[0], slot[1]],
            send_sem=gx_send.at[i, step],
            recv_sem=gx_recv.at[i, step],
            device_id=there,
            device_id_type=MESH,
        )

    def out_copy(i, step, to):
        lead, rest = step // parts, lax.rem(step, parts)
        if to:
            there = (lax.rem(group + lead, groups), lax.rem(part + rest, parts))
            channel = i * devices + me
        else:
            there = (lax.rem(group - lead + groups, groups), lax.rem(part - rest + parts, parts))
            channel = i * devices + there[0] * parts + there[1]
        return pltpu.make_async_remote_copy(
            src_ref=send_out.at[i, there[0], there[1]],
            dst_ref=out_ref.at[channel],
            send_sem=out_send.at[i, step],
            recv_sem=out_recv.at[i, step],
            device_id=there,
            device_id_type=MESH,
        )

    for i in range(count):
        pl.loop(1, parts)(lambda step: filter_copy(i, step, True).start())
        pl.loop(1, devices)(lambda step: row_copy(i, step, True).start())
    for i in range(count):
        recv_gx[i, group, part] = send_gx[i, me]
        recv_f[i, part] = send_f[i, me]

    def product3(left, right):
        (left_high, left_low), (right_high, right_low) = left, right
        return (
            dot(left_high, right_high) + dot(left_low, right_high) + dot(left_high, right_low)
        )

    def turn(real, imag, sine):
        cosine = phi_ref[0]
        return real * cosine - imag * sine, real * sine + imag * cosine

    for i in range(count):
        pl.loop(1, parts)(lambda step: filter_copy(i, step, False).wait_recv())
        pl.loop(1, devices)(lambda step: row_copy(i, step, False).wait_recv())

        def signal(kind, b):
            return recv_gx[i, b, :, kind].reshape(half, LANES).astype(jnp.bfloat16)

        exact = jnp.concatenate(
            [signal(0, b) for b in range(groups)] + [signal(1, b) for b in range(groups)], axis=1
        )
        high, low = split(recv_f[i].reshape(half, LANES))
        stepped = dot(outer_ref[...], jnp.concatenate([exact, exact], axis=0))
        filter_part = dot(outer3_ref[...], jnp.concatenate([high, high, low], axis=0))
        stepped = jnp.concatenate([stepped, filter_part], axis=1)
        turned = []
        for s in range(2 * groups + 1):
            lanes = slice(s * LANES, (s + 1) * LANES)
            pair = turn(stepped[:half, lanes], stepped[half:, lanes], phi_ref[1])
            turned.append(jnp.concatenate(pair, axis=1))
        spec = product3(split(jnp.concatenate(turned, axis=0)), (inner_ref[0], inner_ref[1]))

        def piece(s):
            block = spec[s * half:(s + 1) * half]
            return block[:, :LANES], block[:, LANES:]

        filter_spec = piece(2 * groups)
        products = []
        total = None
        for b in range(groups):
            grad_spec, input_spec = piece(b), piece(groups + b)
            for first in (filter_spec, input_spec):
                term = jnp.concatenate(
                    [
                        first[0] * grad_spec[0] + first[1] * grad_spec[1],
                        first[0] * grad_spec[1] - first[1] * grad_spec[0],
                    ],
                    axis=1,
                )
                if first is filter_spec:
                    products.append(term)
                else:
                    total = term if total is None else total + term
        products.append(total)
        folded = product3(split(jnp.concatenate(products, axis=0)), (inner_t_ref[0], inner_t_ref[1]))
        turned = []
        for s in range(groups + 1):
            block = folded[s * half:(s + 1) * half]
            pair = turn(block[:, :LANES], block[:, LANES:], -phi_ref[1])
            turned.append(jnp.concatenate(pair, axis=0))
        final = product3((back_ref[0], back_ref[1]), split(jnp.concatenate(turned, axis=1)))
        filter_grad = final[:, groups * LANES:].reshape(parts, rows, LANES)
        for b in range(groups):
            through = final[:, b * LANES:(b + 1) * LANES]
            send_out[i, b, :, 0] = through.reshape(parts, rows, LANES)
            send_out[i, b, :, 1] = filter_grad
        pl.loop(1, devices)(lambda step: out_copy(i, step, True).start())
        out_ref[i * devices + me] = send_out[i, group, part]

    for i in range(count):
        pl.loop(1, parts)(lambda step: filter_copy(i, step, True).wait_send())
        pl.loop(1, devices)(lambda step: row_copy(i, step, True).wait_send())
        pl.loop(1, devices)(lambda step: out_copy(i, step, True).wait_send())
        pl.loop(1, devices)(lambda step: out_copy(i, step, False).wait_recv())


def fused_body(groups, parts, inputs, cotangent, filters, skip_gain):
    channels, width = filters.shape
    rows, half = width // LANES, parts * width // LANES
    devices = groups * parts
    count = channels // devices
    outer, phi, inner, back = dft_tables(parts * width)
    outer_high, outer_low = np_split(outer)
    tables = (
        np.concatenate([outer_high, outer_low], axis=1),
        np.concatenate([outer_high, outer_low, outer_high], axis=1),
        phi,
        np.stack(np_split(inner)),
        np.stack(np_split(inner.T)),
        np.stack(np_split(back)),
    )
    tile = (rows, LANES)
    out = pl.pallas_call(
        functools.partial(kernel, groups, parts, count, half),
        out_shape=jax.ShapeDtypeStruct((channels, 2) + tile, jnp.float32),
        in_specs=[pl.BlockSpec(memory_space=pltpu.VMEM)] * 9,
        out_specs=pl.BlockSpec(memory_space=pltpu.VMEM),
        scratch_shapes=[
            pltpu.VMEM((count, devices, 2) + tile, jnp.float32),
            pltpu.VMEM((count, devices) + tile, jnp.float32),
            pltpu.VMEM((count, groups, parts, 2) + tile, jnp.float32),
            pltpu.VMEM((count, parts) + tile, jnp.float32),
            pltpu.VMEM((count, groups, parts, 2) + tile, jnp.float32),
            pltpu.SemaphoreType.DMA((count, devices)),
            pltpu.SemaphoreType.DMA((count, devices)),
            pltpu.SemaphoreType.DMA((count, parts)),
            pltpu.SemaphoreType.DMA((count, parts)),
            pltpu.SemaphoreType.DMA((count, devices)),
            pltpu.SemaphoreType.DMA((count, devices)),
        ],
        compiler_params=pltpu.CompilerParams(
            collective_id=0, has_side_effects=True, vmem_limit_bytes=40 * 2**20
        ),
    )(inputs, cotangent, filters, *(jnp.asarray(t) for t in tables))
    through = out[:, 0].reshape(channels, width)
    input_grad = through + skip_gain[:, None] * cotangent[0].astype(jnp.float32)
    return input_grad.astype(jnp.bfloat16)[None], out[:, 1].reshape(channels, width)


def solution(mesh):
    groups, parts = mesh.shape["dp"], mesh.shape["ctx"]

    def body(inputs, cotangent, filters, skip_gain):
        if filters.shape[0] % (groups * parts) or inputs.shape[0] != 1:
            return plain_body(inputs, cotangent, filters, skip_gain)
        return fused_body(groups, parts, inputs, cotangent, filters, skip_gain)

    return jax.shard_map(
        body,
        mesh=mesh,
        in_specs=(P("dp", None, "ctx"), P("dp", None, "ctx"), P(None, "ctx"), P()),
        out_specs=(P("dp", None, "ctx"), P(None, "ctx")),
        check_vma=False,
    )
```

```python
import functools
import math

import jax
import jax.numpy as jnp
import ml_dtypes
import numpy as np
from jax import lax
from jax.experimental import pallas as pl
from jax.experimental.pallas import tpu as pltpu
from jax.sharding import PartitionSpec as P

LANES = 128
MESH = pl.DeviceIdType.MESH


def dft_tables(length):
    half = length // LANES
    row = np.arange(half)
    lane = np.arange(LANES)
    theta = 2 * math.pi / (2 * half) * (((row[:, None] + 0.5) * row[None, :]) % (2 * half))
    outer = np.concatenate([np.cos(theta), -np.sin(theta)])
    phi = math.pi / length * ((row[:, None] + 0.5) * lane[None, :])
    phi_table = np.stack([np.cos(phi), -np.sin(phi)])
    psi = 2 * math.pi / LANES * ((lane[:, None] * lane[None, :]) % LANES)
    cos, sin = np.cos(psi), np.sin(psi)
    inner = np.block([[cos, -sin], [sin, cos]])
    back = outer.T / length / math.sqrt(length)
    return outer, phi_table.astype(np.float32), inner, back


def np_split(table):
    high = table.astype(ml_dtypes.bfloat16)
    low = (table - high.astype(np.float64)).astype(ml_dtypes.bfloat16)
    return high, low


def split(values):
    high = values.astype(jnp.bfloat16)
    return high, (values - high.astype(jnp.float32)).astype(jnp.bfloat16)


def dot(left, right):
    return jnp.dot(left, right, preferred_element_type=jnp.float32)


def plain_gradients(grads, inputs, filters):
    batch, channels, length = grads.shape
    half = length // LANES
    outer, phi, inner, back = dft_tables(length)
    outer, inner, back = (t.astype(np.float32) for t in (outer, inner, back))
    product = functools.partial(jnp.matmul, precision=lax.Precision.HIGHEST)

    def forward(values):
        rows = product(outer, values.reshape(values.shape[:-1] + (half, LANES)))
        real, imag = rows[..., :half, :], rows[..., half:, :]
        turned = jnp.concatenate(
            [real * phi[0] - imag * phi[1], real * phi[1] + imag * phi[0]], axis=-1
        )
        spec = product(turned, inner)
        return spec[..., :LANES], spec[..., LANES:]

    def backward(real, imag):
        rows = product(jnp.concatenate([real, imag], axis=-1), inner.T)
        real, imag = rows[..., :LANES], rows[..., LANES:]
        turned = jnp.concatenate(
            [real * phi[0] + imag * phi[1], imag * phi[0] - real * phi[1]], axis=-2
        )
        out = product(back, turned)
        return out.reshape(out.shape[:-2] + (length,))

    def conj_product(first, second):
        return (
            first[0] * second[0] + first[1] * second[1],
            first[0] * second[1] - first[1] * second[0],
        )

    grad_spec = forward(grads)
    through = backward(*conj_product(forward(filters), grad_spec))
    real, imag = conj_product(forward(inputs), grad_spec)
    return through, backward(real.sum(0), imag.sum(0))


def plain_body(inputs, cotangent, filters, skip_gain):
    def gather(values):
        return lax.all_to_all(values, "ctx", 0, 1, tiled=True)

    grad_rows = cotangent[0].astype(jnp.float32)
    grads, rows = gather(grad_rows), gather(inputs[0].astype(jnp.float32))
    through, filter_grad = plain_gradients(grads[None], rows[None], gather(filters))
    filter_grad = lax.psum(filter_grad, "dp")
    through = lax.all_to_all(through[0], "ctx", 1, 0, tiled=True)
    filter_grad = lax.all_to_all(filter_grad, "ctx", 1, 0, tiled=True)
    return (through + skip_gain[:, None] * grad_rows).astype(jnp.bfloat16)[None], filter_grad


def kernel(
    groups, parts, count, half,
    x_hbm, g_hbm, f_hbm, outer_hbm, outer3_hbm, phi_hbm, inner_hbm, inner_t_hbm, back_hbm,
    out_ref,
    x_ref, g_ref, f_ref, outer_ref, outer3_ref, phi_ref, inner_ref, inner_t_ref, back_ref,
    send_gx, send_f, recv_gx, recv_f, send_out,
    load_sem, gx_send, gx_recv, f_send, f_recv, out_send, out_recv,
):
    devices = groups * parts
    rows = x_ref.shape[2] // LANES
    group, part = lax.axis_index("dp"), lax.axis_index("ctx")
    me = group * parts + part

    loads = [
        pltpu.make_async_copy(source, target, load_sem.at[n])
        for n, (source, target) in enumerate(
            [
                (g_hbm, g_ref), (x_hbm, x_ref), (f_hbm, f_ref),
                (outer_hbm, outer_ref), (outer3_hbm, outer3_ref), (phi_hbm, phi_ref),
                (inner_hbm, inner_ref), (inner_t_hbm, inner_t_ref), (back_hbm, back_ref),
            ]
        )
    ]
    for load in loads:
        load.start()

    barrier = pltpu.get_barrier_semaphore()

    @pl.loop(1, devices)
    def _(step):
        other = lax.rem(me + step, devices)
        pl.semaphore_signal(
            barrier, inc=1, device_id=(other // parts, lax.rem(other, parts)),
            device_id_type=MESH,
        )

    for load in loads[:3]:
        load.wait()
    for i in range(count):
        own = slice(i * devices, (i + 1) * devices)
        for r in range(rows):
            lanes = slice(r * LANES, (r + 1) * LANES)
            send_gx[i, :, 0, r, :] = g_ref[0, own, lanes].astype(jnp.float32)
            send_gx[i, :, 1, r, :] = x_ref[0, own, lanes].astype(jnp.float32)
            send_f[i, :, r, :] = f_ref[own, lanes]

    pl.semaphore_wait(barrier, devices - 1)

    def filter_copy(i, step, to):
        other = lax.rem(part + step, parts) if to else lax.rem(part - step + parts, parts)
        return pltpu.make_async_remote_copy(
            src_ref=send_f.at[i, group * parts + other],
            dst_ref=recv_f.at[i, part if to else other],
            send_sem=f_send.at[i, step],
            recv_sem=f_recv.at[i, step],
            device_id=(group, other),
            device_id_type=MESH,
        )

    def row_copy(i, step, to):
        lead, rest = step // parts, lax.rem(step, parts)
        if to:
            there = (lax.rem(group + lead, groups), lax.rem(part + rest, parts))
            slot = (group, part)
        else:
            there = (lax.rem(group - lead + groups, groups), lax.rem(part - rest + parts, parts))
            slot = there
        return pltpu.make_async_remote_copy(
            src_ref=send_gx.at[i, there[0] * parts + there[1]],
            dst_ref=recv_gx.at[i, slot[0], slot[1]],
            send_sem=gx_send.at[i, step],
            recv_sem=gx_recv.at[i, step],
            device_id=there,
            device_id_type=MESH,
        )

    def out_copy(i, step, to):
        lead, rest = step // parts, lax.rem(step, parts)
        if to:
            there = (lax.rem(group + lead, groups), lax.rem(part + rest, parts))
            channel = i * devices + me
        else:
            there = (lax.rem(group - lead + groups, groups), lax.rem(part - rest + parts, parts))
            channel = i * devices + there[0] * parts + there[1]
        return pltpu.make_async_remote_copy(
            src_ref=send_out.at[i, there[0], there[1]],
            dst_ref=out_ref.at[channel],
            send_sem=out_send.at[i, step],
            recv_sem=out_recv.at[i, step],
            device_id=there,
            device_id_type=MESH,
        )

    for i in range(count):
        pl.loop(1, parts)(lambda step: filter_copy(i, step, True).start())
        pl.loop(1, devices)(lambda step: row_copy(i, step, True).start())
    for i in range(count):
        recv_gx[i, group, part] = send_gx[i, me]
        recv_f[i, part] = send_f[i, me]

    for load in loads[3:]:
        load.wait()

    def product3(left, right):
        (left_high, left_low), (right_high, right_low) = left, right
        return (
            dot(left_high, right_high) + dot(left_low, right_high) + dot(left_high, right_low)
        )

    def turn(real, imag, sine):
        cosine = phi_ref[0]
        return real * cosine - imag * sine, real * sine + imag * cosine

    for i in range(count):
        pl.loop(1, parts)(lambda step: filter_copy(i, step, False).wait_recv())
        pl.loop(1, devices)(lambda step: row_copy(i, step, False).wait_recv())

        def signal(kind, b):
            return recv_gx[i, b, :, kind].reshape(half, LANES).astype(jnp.bfloat16)

        exact = jnp.concatenate(
            [signal(0, b) for b in range(groups)] + [signal(1, b) for b in range(groups)], axis=1
        )
        high, low = split(recv_f[i].reshape(half, LANES))
        stepped = dot(outer_ref[...], jnp.concatenate([exact, exact], axis=0))
        filter_part = dot(outer3_ref[...], jnp.concatenate([high, high, low], axis=0))
        stepped = jnp.concatenate([stepped, filter_part], axis=1)
        turned = []
        for s in range(2 * groups + 1):
            lanes = slice(s * LANES, (s + 1) * LANES)
            pair = turn(stepped[:half, lanes], stepped[half:, lanes], phi_ref[1])
            turned.append(jnp.concatenate(pair, axis=1))
        spec = product3(split(jnp.concatenate(turned, axis=0)), (inner_ref[0], inner_ref[1]))

        def piece(s):
            block = spec[s * half:(s + 1) * half]
            return block[:, :LANES], block[:, LANES:]

        filter_spec = piece(2 * groups)
        products = []
        total = None
        for b in range(groups):
            grad_spec, input_spec = piece(b), piece(groups + b)
            for first in (filter_spec, input_spec):
                term = jnp.concatenate(
                    [
                        first[0] * grad_spec[0] + first[1] * grad_spec[1],
                        first[0] * grad_spec[1] - first[1] * grad_spec[0],
                    ],
                    axis=1,
                )
                if first is filter_spec:
                    products.append(term)
                else:
                    total = term if total is None else total + term
        products.append(total)
        folded = product3(split(jnp.concatenate(products, axis=0)), (inner_t_ref[0], inner_t_ref[1]))
        turned = []
        for s in range(groups + 1):
            block = folded[s * half:(s + 1) * half]
            pair = turn(block[:, :LANES], block[:, LANES:], -phi_ref[1])
            turned.append(jnp.concatenate(pair, axis=0))
        final = product3((back_ref[0], back_ref[1]), split(jnp.concatenate(turned, axis=1)))
        filter_grad = final[:, groups * LANES:].reshape(parts, rows, LANES)
        for b in range(groups):
            through = final[:, b * LANES:(b + 1) * LANES]
            send_out[i, b, :, 0] = through.reshape(parts, rows, LANES)
            send_out[i, b, :, 1] = filter_grad
        pl.loop(1, devices)(lambda step: out_copy(i, step, True).start())
        out_ref[i * devices + me] = send_out[i, group, part]

    for i in range(count):
        pl.loop(1, parts)(lambda step: filter_copy(i, step, True).wait_send())
        pl.loop(1, devices)(lambda step: row_copy(i, step, True).wait_send())
        pl.loop(1, devices)(lambda step: out_copy(i, step, True).wait_send())
        pl.loop(1, devices)(lambda step: out_copy(i, step, False).wait_recv())


def fused_body(groups, parts, inputs, cotangent, filters, skip_gain):
    channels, width = filters.shape
    rows, half = width // LANES, parts * width // LANES
    devices = groups * parts
    count = channels // devices
    outer, phi, inner, back = dft_tables(parts * width)
    outer_high, outer_low = np_split(outer)
    tables = (
        np.concatenate([outer_high, outer_low], axis=1),
        np.concatenate([outer_high, outer_low, outer_high], axis=1),
        phi,
        np.stack(np_split(inner)),
        np.stack(np_split(inner.T)),
        np.stack(np_split(back)),
    )
    tables = tuple(jnp.asarray(t) for t in tables)
    operands = (inputs, cotangent, filters) + tables
    tile = (rows, LANES)
    out = pl.pallas_call(
        functools.partial(kernel, groups, parts, count, half),
        out_shape=jax.ShapeDtypeStruct((channels, 2) + tile, jnp.float32),
        in_specs=[pl.BlockSpec(memory_space=pltpu.HBM)] * 9,
        out_specs=pl.BlockSpec(memory_space=pltpu.VMEM),
        scratch_shapes=[pltpu.VMEM(t.shape, t.dtype) for t in operands] + [
            pltpu.VMEM((count, devices, 2) + tile, jnp.float32),
            pltpu.VMEM((count, devices) + tile, jnp.float32),
            pltpu.VMEM((count, groups, parts, 2) + tile, jnp.float32),
            pltpu.VMEM((count, parts) + tile, jnp.float32),
            pltpu.VMEM((count, groups, parts, 2) + tile, jnp.float32),
            pltpu.SemaphoreType.DMA((len(operands),)),
            pltpu.SemaphoreType.DMA((count, devices)),
            pltpu.SemaphoreType.DMA((count, devices)),
            pltpu.SemaphoreType.DMA((count, parts)),
            pltpu.SemaphoreType.DMA((count, parts)),
            pltpu.SemaphoreType.DMA((count, devices)),
            pltpu.SemaphoreType.DMA((count, devices)),
        ],
        compiler_params=pltpu.CompilerParams(
            collective_id=0, has_side_effects=True, vmem_limit_bytes=40 * 2**20
        ),
    )(*operands)
    through = out[:, 0].reshape(channels, width)
    input_grad = through + skip_gain[:, None] * cotangent[0].astype(jnp.float32)
    return input_grad.astype(jnp.bfloat16)[None], out[:, 1].reshape(channels, width)


def solution(mesh):
    groups, parts = mesh.shape["dp"], mesh.shape["ctx"]

    def body(inputs, cotangent, filters, skip_gain):
        if filters.shape[0] % (groups * parts) or inputs.shape[0] != 1:
            return plain_body(inputs, cotangent, filters, skip_gain)
        return fused_body(groups, parts, inputs, cotangent, filters, skip_gain)

    return jax.shard_map(
        body,
        mesh=mesh,
        in_specs=(P("dp", None, "ctx"), P("dp", None, "ctx"), P(None, "ctx"), P()),
        out_specs=(P("dp", None, "ctx"), P(None, "ctx")),
        check_vma=False,
    )
```

```python
import functools
import math

import jax
import jax.numpy as jnp
import ml_dtypes
import numpy as np
from jax import lax
from jax.experimental import pallas as pl
from jax.experimental.pallas import tpu as pltpu
from jax.sharding import PartitionSpec as P

LANES = 128
MESH = pl.DeviceIdType.MESH


def dft_tables(length):
    half = length // LANES
    row = np.arange(half)
    lane = np.arange(LANES)
    theta = 2 * math.pi / (2 * half) * (((row[:, None] + 0.5) * row[None, :]) % (2 * half))
    outer = np.concatenate([np.cos(theta), -np.sin(theta)])
    phi = math.pi / length * ((row[:, None] + 0.5) * lane[None, :])
    phi_table = np.stack([np.cos(phi), -np.sin(phi)])
    psi = 2 * math.pi / LANES * ((lane[:, None] * lane[None, :]) % LANES)
    cos, sin = np.cos(psi), np.sin(psi)
    inner = np.block([[cos, -sin], [sin, cos]])
    back = outer.T / length / math.sqrt(length)
    return outer, phi_table.astype(np.float32), inner, back


def np_split(table):
    high = table.astype(ml_dtypes.bfloat16)
    low = (table - high.astype(np.float64)).astype(ml_dtypes.bfloat16)
    return high, low


def split(values):
    high = values.astype(jnp.bfloat16)
    return high, (values - high.astype(jnp.float32)).astype(jnp.bfloat16)


def dot(left, right):
    return jnp.dot(left, right, preferred_element_type=jnp.float32)


def plain_gradients(grads, inputs, filters):
    batch, channels, length = grads.shape
    half = length // LANES
    outer, phi, inner, back = dft_tables(length)
    outer, inner, back = (t.astype(np.float32) for t in (outer, inner, back))
    product = functools.partial(jnp.matmul, precision=lax.Precision.HIGHEST)

    def forward(values):
        rows = product(outer, values.reshape(values.shape[:-1] + (half, LANES)))
        real, imag = rows[..., :half, :], rows[..., half:, :]
        turned = jnp.concatenate(
            [real * phi[0] - imag * phi[1], real * phi[1] + imag * phi[0]], axis=-1
        )
        spec = product(turned, inner)
        return spec[..., :LANES], spec[..., LANES:]

    def backward(real, imag):
        rows = product(jnp.concatenate([real, imag], axis=-1), inner.T)
        real, imag = rows[..., :LANES], rows[..., LANES:]
        turned = jnp.concatenate(
            [real * phi[0] + imag * phi[1], imag * phi[0] - real * phi[1]], axis=-2
        )
        out = product(back, turned)
        return out.reshape(out.shape[:-2] + (length,))

    def conj_product(first, second):
        return (
            first[0] * second[0] + first[1] * second[1],
            first[0] * second[1] - first[1] * second[0],
        )

    grad_spec = forward(grads)
    through = backward(*conj_product(forward(filters), grad_spec))
    real, imag = conj_product(forward(inputs), grad_spec)
    return through, backward(real.sum(0), imag.sum(0))


def plain_body(inputs, cotangent, filters, skip_gain):
    def gather(values):
        return lax.all_to_all(values, "ctx", 0, 1, tiled=True)

    grad_rows = cotangent[0].astype(jnp.float32)
    grads, rows = gather(grad_rows), gather(inputs[0].astype(jnp.float32))
    through, filter_grad = plain_gradients(grads[None], rows[None], gather(filters))
    filter_grad = lax.psum(filter_grad, "dp")
    through = lax.all_to_all(through[0], "ctx", 1, 0, tiled=True)
    filter_grad = lax.all_to_all(filter_grad, "ctx", 1, 0, tiled=True)
    return (through + skip_gain[:, None] * grad_rows).astype(jnp.bfloat16)[None], filter_grad


def kernel(
    groups, parts, count, half,
    x_hbm, g_hbm, f_hbm, outer_hbm, outer3_hbm, phi_hbm, inner_hbm, inner_t_hbm, back_hbm,
    through_ref, filter_grad_ref,
    x_ref, g_ref, f_ref, outer_ref, outer3_ref, phi_ref, inner_ref, inner_t_ref, back_ref,
    send_gx, send_f, recv_gx, recv_f, send_through, send_filter_grad,
    load_sem, gx_sem, f_sem, through_sem, filter_grad_sem, relay_sem,
):
    devices = groups * parts
    rows = x_ref.shape[2] // LANES
    group, part = lax.axis_index("dp"), lax.axis_index("ctx")
    me = group * parts + part

    loads = [
        pltpu.make_async_copy(source, target, load_sem.at[n])
        for n, (source, target) in enumerate(
            [
                (g_hbm, g_ref), (x_hbm, x_ref), (f_hbm, f_ref),
                (outer_hbm, outer_ref), (outer3_hbm, outer3_ref), (phi_hbm, phi_ref),
                (inner_hbm, inner_ref), (inner_t_hbm, inner_t_ref), (back_hbm, back_ref),
            ]
        )
    ]
    for load in loads:
        load.start()

    def after(position, step, size):
        moved = position + step
        return jnp.where(moved >= size, moved - size, moved)

    def each_other(act):
        for lead in range(groups):
            there = after(group, lead, groups)

            @pl.loop(0 if lead else 1, parts)
            def _(step):
                act(there, after(part, step, parts))

    barrier = pltpu.get_barrier_semaphore()
    each_other(
        lambda to_group, to_part: pl.semaphore_signal(
            barrier, inc=1, device_id=(to_group, to_part), device_id_type=MESH
        )
    )

    def remote(source, target, sems, i, to_group, to_part):
        pltpu.make_async_remote_copy(
            src_ref=source,
            dst_ref=target,
            send_sem=sems.at[0, i],
            recv_sem=sems.at[1, i],
            device_id=(to_group, to_part),
            device_id_type=MESH,
        ).start()

    def wait_bytes(held, sem):
        pltpu.make_async_copy(held, held, sem).wait()

    def pack(i):
        own = slice(i * devices, (i + 1) * devices)
        for r in range(rows):
            lanes = slice(r * LANES, (r + 1) * LANES)
            send_gx[i, :, 0, r, :] = g_ref[0, own, lanes].astype(jnp.float32)
            send_gx[i, :, 1, r, :] = x_ref[0, own, lanes].astype(jnp.float32)
            send_f[i, :, r, :] = f_ref[own, lanes]

    def send_rows(i):
        @pl.loop(1, parts)
        def _(step):
            other = after(part, step, parts)
            remote(
                send_f.at[i, group * parts + other], recv_f.at[i, part], f_sem, i, group, other
            )

        each_other(
            lambda to_group, to_part: remote(
                send_gx.at[i, to_group * parts + to_part], recv_gx.at[i, me],
                gx_sem, i, to_group, to_part,
            )
        )
        recv_gx[i, me] = send_gx[i, me]
        recv_f[i, part] = send_f[i, me]

    for load in loads[:3]:
        load.wait()
    pack(0)
    pl.semaphore_wait(barrier, devices - 1)
    send_rows(0)
    for i in range(1, count):
        pack(i)
        send_rows(i)
    for load in loads[3:]:
        load.wait()

    def product3(left, right):
        (left_high, left_low), (right_high, right_low) = left, right
        return (
            dot(left_high, right_high) + dot(left_low, right_high) + dot(left_high, right_low)
        )

    def turn(real, imag, sine):
        cosine = phi_ref[0]
        return real * cosine - imag * sine, real * sine + imag * cosine

    for i in range(count):
        wait_bytes(recv_f.at[i, pl.ds(0, parts - 1)], f_sem.at[1, i])
        wait_bytes(recv_gx.at[i, pl.ds(0, devices - 1)], gx_sem.at[1, i])

        def signal(kind, b):
            return recv_gx[i, b * parts:(b + 1) * parts, kind].reshape(half, LANES).astype(jnp.bfloat16)

        exact = jnp.concatenate(
            [signal(0, b) for b in range(groups)] + [signal(1, b) for b in range(groups)], axis=1
        )
        high, low = split(recv_f[i].reshape(half, LANES))
        stepped = dot(outer_ref[...], jnp.concatenate([exact, exact], axis=0))
        filter_part = dot(outer3_ref[...], jnp.concatenate([high, high, low], axis=0))
        stepped = jnp.concatenate([stepped, filter_part], axis=1)
        turned = []
        for s in range(2 * groups + 1):
            lanes = slice(s * LANES, (s + 1) * LANES)
            pair = turn(stepped[:half, lanes], stepped[half:, lanes], phi_ref[1])
            turned.append(jnp.concatenate(pair, axis=1))
        spec = product3(split(jnp.concatenate(turned, axis=0)), (inner_ref[0], inner_ref[1]))

        def piece(s):
            block = spec[s * half:(s + 1) * half]
            return block[:, :LANES], block[:, LANES:]

        filter_spec = piece(2 * groups)
        products = []
        total = None
        for b in range(groups):
            grad_spec, input_spec = piece(b), piece(groups + b)
            for first in (filter_spec, input_spec):
                term = jnp.concatenate(
                    [
                        first[0] * grad_spec[0] + first[1] * grad_spec[1],
                        first[0] * grad_spec[1] - first[1] * grad_spec[0],
                    ],
                    axis=1,
                )
                if first is filter_spec:
                    products.append(term)
                else:
                    total = term if total is None else total + term
        products.append(total)
        folded = product3(split(jnp.concatenate(products, axis=0)), (inner_t_ref[0], inner_t_ref[1]))
        turned = []
        for s in range(groups + 1):
            block = folded[s * half:(s + 1) * half]
            pair = turn(block[:, :LANES], block[:, LANES:], -phi_ref[1])
            turned.append(jnp.concatenate(pair, axis=0))
        final = product3((back_ref[0], back_ref[1]), split(jnp.concatenate(turned, axis=1)))
        send_filter_grad[i] = final[:, groups * LANES:].reshape(parts, rows, LANES)
        for b in range(groups):
            through = final[:, b * LANES:(b + 1) * LANES]
            send_through[i, b * parts:(b + 1) * parts] = through.reshape(parts, rows, LANES)

        channel = i * devices + me

        @pl.loop(1, parts)
        def _(step):
            other = after(part, step, parts)
            remote(
                send_filter_grad.at[i, other], filter_grad_ref.at[channel],
                filter_grad_sem, i, group, other,
            )

        each_other(
            lambda to_group, to_part: remote(
                send_through.at[i, to_group * parts + to_part], through_ref.at[channel],
                through_sem, i, to_group, to_part,
            )
        )
        filter_grad_ref[channel] = send_filter_grad[i, part]
        through_ref[channel] = send_through[i, me]

    def held_by(i, b):
        return filter_grad_ref.at[pl.ds(i * devices + b * parts, parts)]

    for i in range(count):
        wait_bytes(
            filter_grad_ref.at[pl.ds(i * devices, parts - 1)], filter_grad_sem.at[1, i]
        )
        for lead in range(1, groups):
            remote(
                held_by(i, group), held_by(i, group), relay_sem, i, after(group, lead, groups), part
            )

    for i in range(count):
        wait_bytes(send_f.at[i, pl.ds(0, parts - 1)], f_sem.at[0, i])
        wait_bytes(send_gx.at[i, pl.ds(0, devices - 1)], gx_sem.at[0, i])
        wait_bytes(send_filter_grad.at[i, pl.ds(0, parts - 1)], filter_grad_sem.at[0, i])
        for side in range(2):
            wait_bytes(send_through.at[i, pl.ds(0, devices - 1)], through_sem.at[side, i])
            relayed = pl.ds(i * devices, (groups - 1) * parts)
            wait_bytes(filter_grad_ref.at[relayed], relay_sem.at[side, i])


def fused_body(groups, parts, inputs, cotangent, filters, skip_gain):
    channels, width = filters.shape
    rows, half = width // LANES, parts * width // LANES
    devices = groups * parts
    count = channels // devices
    outer, phi, inner, back = dft_tables(parts * width)
    outer_high, outer_low = np_split(outer)
    tables = (
        np.concatenate([outer_high, outer_low], axis=1),
        np.concatenate([outer_high, outer_low, outer_high], axis=1),
        phi,
        np.stack(np_split(inner)),
        np.stack(np_split(inner.T)),
        np.stack(np_split(back)),
    )
    tables = tuple(jnp.asarray(t) for t in tables)
    operands = (inputs, cotangent, filters) + tables
    tile = (rows, LANES)
    whole = jax.ShapeDtypeStruct((channels,) + tile, jnp.float32)
    through, filter_grad = pl.pallas_call(
        functools.partial(kernel, groups, parts, count, half),
        out_shape=(whole, whole),
        in_specs=[pl.BlockSpec(memory_space=pltpu.HBM)] * len(operands),
        out_specs=(pl.BlockSpec(memory_space=pltpu.VMEM),) * 2,
        scratch_shapes=[pltpu.VMEM(t.shape, t.dtype) for t in operands] + [
            pltpu.VMEM((count, devices, 2) + tile, jnp.float32),
            pltpu.VMEM((count, devices) + tile, jnp.float32),
            pltpu.VMEM((count, devices, 2) + tile, jnp.float32),
            pltpu.VMEM((count, parts) + tile, jnp.float32),
            pltpu.VMEM((count, devices) + tile, jnp.float32),
            pltpu.VMEM((count, parts) + tile, jnp.float32),
            pltpu.SemaphoreType.DMA((len(operands),)),
        ] + [pltpu.SemaphoreType.DMA((2, count))] * 5,
        compiler_params=pltpu.CompilerParams(collective_id=0, has_side_effects=True),
    )(*operands)
    through = through.reshape(channels, width)
    input_grad = through + skip_gain[:, None] * cotangent[0].astype(jnp.float32)
    return input_grad.astype(jnp.bfloat16)[None], filter_grad.reshape(channels, width)


def solution(mesh):
    groups, parts = mesh.shape["dp"], mesh.shape["ctx"]

    def body(inputs, cotangent, filters, skip_gain):
        if filters.shape[0] % (groups * parts) or inputs.shape[0] != 1:
            return plain_body(inputs, cotangent, filters, skip_gain)
        return fused_body(groups, parts, inputs, cotangent, filters, skip_gain)

    return jax.shard_map(
        body,
        mesh=mesh,
        in_specs=(P("dp", None, "ctx"), P("dp", None, "ctx"), P(None, "ctx"), P()),
        out_specs=(P("dp", None, "ctx"), P(None, "ctx")),
        check_vma=False,
    )
```

```python
import functools
import math

import jax
import jax.numpy as jnp
import ml_dtypes
import numpy as np
from jax import lax
from jax.experimental import pallas as pl
from jax.experimental.pallas import tpu as pltpu
from jax.sharding import PartitionSpec as P

LANES = 128
MESH = pl.DeviceIdType.MESH


def dft_tables(length):
    half = length // LANES
    row = np.arange(half)
    lane = np.arange(LANES)
    theta = 2 * math.pi / (2 * half) * (((row[:, None] + 0.5) * row[None, :]) % (2 * half))
    outer = np.concatenate([np.cos(theta), -np.sin(theta)])
    phi = math.pi / length * ((row[:, None] + 0.5) * lane[None, :])
    phi_table = np.stack([np.cos(phi), -np.sin(phi)])
    psi = 2 * math.pi / LANES * ((lane[:, None] * lane[None, :]) % LANES)
    cos, sin = np.cos(psi), np.sin(psi)
    inner = np.block([[cos, -sin], [sin, cos]])
    back = outer.T / length / math.sqrt(length)
    return outer, phi_table.astype(np.float32), inner, back


def np_split(table):
    high = table.astype(ml_dtypes.bfloat16)
    low = (table - high.astype(np.float64)).astype(ml_dtypes.bfloat16)
    return high, low


def split(values):
    high = values.astype(jnp.bfloat16)
    return high, (values - high.astype(jnp.float32)).astype(jnp.bfloat16)


def dot(left, right):
    return jnp.dot(left, right, preferred_element_type=jnp.float32)


def plain_gradients(grads, inputs, filters):
    batch, channels, length = grads.shape
    half = length // LANES
    outer, phi, inner, back = dft_tables(length)
    outer, inner, back = (t.astype(np.float32) for t in (outer, inner, back))
    product = functools.partial(jnp.matmul, precision=lax.Precision.HIGHEST)

    def forward(values):
        rows = product(outer, values.reshape(values.shape[:-1] + (half, LANES)))
        real, imag = rows[..., :half, :], rows[..., half:, :]
        turned = jnp.concatenate(
            [real * phi[0] - imag * phi[1], real * phi[1] + imag * phi[0]], axis=-1
        )
        spec = product(turned, inner)
        return spec[..., :LANES], spec[..., LANES:]

    def backward(real, imag):
        rows = product(jnp.concatenate([real, imag], axis=-1), inner.T)
        real, imag = rows[..., :LANES], rows[..., LANES:]
        turned = jnp.concatenate(
            [real * phi[0] + imag * phi[1], imag * phi[0] - real * phi[1]], axis=-2
        )
        out = product(back, turned)
        return out.reshape(out.shape[:-2] + (length,))

    def conj_product(first, second):
        return (
            first[0] * second[0] + first[1] * second[1],
            first[0] * second[1] - first[1] * second[0],
        )

    grad_spec = forward(grads)
    through = backward(*conj_product(forward(filters), grad_spec))
    real, imag = conj_product(forward(inputs), grad_spec)
    return through, backward(real.sum(0), imag.sum(0))


def plain_body(inputs, cotangent, filters, skip_gain):
    def gather(values):
        return lax.all_to_all(values, "ctx", 0, 1, tiled=True)

    grad_rows = cotangent[0].astype(jnp.float32)
    grads, rows = gather(grad_rows), gather(inputs[0].astype(jnp.float32))
    through, filter_grad = plain_gradients(grads[None], rows[None], gather(filters))
    filter_grad = lax.psum(filter_grad, "dp")
    through = lax.all_to_all(through[0], "ctx", 1, 0, tiled=True)
    filter_grad = lax.all_to_all(filter_grad, "ctx", 1, 0, tiled=True)
    return (through + skip_gain[:, None] * grad_rows).astype(jnp.bfloat16)[None], filter_grad


def kernel(
    groups, parts, count, half,
    x_hbm, g_hbm, f_hbm, outer_hbm, outer3_hbm, phi_hbm, inner_hbm, inner_t_hbm, back_hbm,
    through_ref, filter_grad_ref,
    x_ref, g_ref, f_ref, outer_ref, outer3_ref, phi_ref, inner_ref, inner_t_ref, back_ref,
    send_gx, send_f, recv_gx, recv_f, send_through, send_filter_grad,
    load_sem, gx_sem, f_sem, through_sem, filter_grad_sem, relay_sem,
):
    devices = groups * parts
    rows = x_ref.shape[2] // LANES
    group, part = lax.axis_index("dp"), lax.axis_index("ctx")
    me = group * parts + part

    loads = [
        pltpu.make_async_copy(source, target, load_sem.at[n])
        for n, (source, target) in enumerate(
            [
                (g_hbm, g_ref), (x_hbm, x_ref), (f_hbm, f_ref),
                (outer_hbm, outer_ref), (outer3_hbm, outer3_ref), (phi_hbm, phi_ref),
                (inner_hbm, inner_ref), (inner_t_hbm, inner_t_ref), (back_hbm, back_ref),
            ]
        )
    ]
    for load in loads:
        load.start()

    def after(position, step, size):
        moved = position + step
        return jnp.where(moved >= size, moved - size, moved)

    def each_other(act):
        for lead in range(groups):
            there = after(group, lead, groups)

            @pl.loop(0 if lead else 1, parts)
            def _(step):
                act(there, after(part, step, parts))

    barrier = pltpu.get_barrier_semaphore()
    each_other(
        lambda to_group, to_part: pl.semaphore_signal(
            barrier, inc=1, device_id=(to_group, to_part), device_id_type=MESH
        )
    )

    def remote(source, target, send_sem, recv_sem, to_group, to_part):
        pltpu.make_async_remote_copy(
            src_ref=source,
            dst_ref=target,
            send_sem=send_sem,
            recv_sem=recv_sem,
            device_id=(to_group, to_part),
            device_id_type=MESH,
        ).start()

    def wait_bytes(held, sem):
        pltpu.make_async_copy(held, held, sem).wait()

    def pack(i):
        own = slice(i * devices, (i + 1) * devices)
        for r in range(rows):
            lanes = slice(r * LANES, (r + 1) * LANES)
            send_gx[:, i, 0, r, :] = g_ref[0, own, lanes].astype(jnp.float32)
            send_gx[:, i, 1, r, :] = x_ref[0, own, lanes].astype(jnp.float32)
            send_f[:, i, r, :] = f_ref[own, lanes]

    for load in loads[:3]:
        load.wait()
    for i in range(count):
        pack(i)
    pl.semaphore_wait(barrier, devices - 1)

    @pl.loop(1, parts)
    def _(step):
        other = after(part, step, parts)
        remote(
            send_f.at[group * parts + other], recv_f.at[part],
            f_sem.at[0], f_sem.at[1], group, other,
        )

    each_other(
        lambda to_group, to_part: remote(
            send_gx.at[to_group * parts + to_part], recv_gx.at[me],
            gx_sem.at[0], gx_sem.at[1], to_group, to_part,
        )
    )
    recv_gx[me] = send_gx[me]
    recv_f[part] = send_f[me]
    for load in loads[3:]:
        load.wait()

    def product3(left, right):
        (left_high, left_low), (right_high, right_low) = left, right
        return (
            dot(left_high, right_high) + dot(left_low, right_high) + dot(left_high, right_low)
        )

    def turn(real, imag, sine):
        cosine = phi_ref[0]
        return real * cosine - imag * sine, real * sine + imag * cosine

    wait_bytes(recv_f.at[pl.ds(0, parts - 1)], f_sem.at[1])
    wait_bytes(recv_gx.at[pl.ds(0, devices - 1)], gx_sem.at[1])

    for i in range(count):

        def signal(kind, b):
            return recv_gx[b * parts:(b + 1) * parts, i, kind].reshape(half, LANES).astype(jnp.bfloat16)

        exact = jnp.concatenate(
            [signal(0, b) for b in range(groups)] + [signal(1, b) for b in range(groups)], axis=1
        )
        high, low = split(recv_f[:, i].reshape(half, LANES))
        stepped = dot(outer_ref[...], jnp.concatenate([exact, exact], axis=0))
        filter_part = dot(outer3_ref[...], jnp.concatenate([high, high, low], axis=0))
        stepped = jnp.concatenate([stepped, filter_part], axis=1)
        turned = []
        for s in range(2 * groups + 1):
            lanes = slice(s * LANES, (s + 1) * LANES)
            pair = turn(stepped[:half, lanes], stepped[half:, lanes], phi_ref[1])
            turned.append(jnp.concatenate(pair, axis=1))
        spec = product3(split(jnp.concatenate(turned, axis=0)), (inner_ref[0], inner_ref[1]))

        def piece(s):
            block = spec[s * half:(s + 1) * half]
            return block[:, :LANES], block[:, LANES:]

        filter_spec = piece(2 * groups)
        products = []
        total = None
        for b in range(groups):
            grad_spec, input_spec = piece(b), piece(groups + b)
            for first in (filter_spec, input_spec):
                term = jnp.concatenate(
                    [
                        first[0] * grad_spec[0] + first[1] * grad_spec[1],
                        first[0] * grad_spec[1] - first[1] * grad_spec[0],
                    ],
                    axis=1,
                )
                if first is filter_spec:
                    products.append(term)
                else:
                    total = term if total is None else total + term
        products.append(total)
        folded = product3(split(jnp.concatenate(products, axis=0)), (inner_t_ref[0], inner_t_ref[1]))
        turned = []
        for s in range(groups + 1):
            block = folded[s * half:(s + 1) * half]
            pair = turn(block[:, :LANES], block[:, LANES:], -phi_ref[1])
            turned.append(jnp.concatenate(pair, axis=0))
        final = product3((back_ref[0], back_ref[1]), split(jnp.concatenate(turned, axis=1)))
        send_filter_grad[i] = final[:, groups * LANES:].reshape(parts, rows, LANES)
        for b in range(groups):
            through = final[:, b * LANES:(b + 1) * LANES]
            send_through[i, b * parts:(b + 1) * parts] = through.reshape(parts, rows, LANES)

        channel = i * devices + me

        @pl.loop(1, parts)
        def _(step):
            other = after(part, step, parts)
            remote(
                send_filter_grad.at[i, other], filter_grad_ref.at[channel],
                filter_grad_sem.at[0, i], filter_grad_sem.at[1, i], group, other,
            )

        each_other(
            lambda to_group, to_part: remote(
                send_through.at[i, to_group * parts + to_part], through_ref.at[channel],
                through_sem.at[0, i], through_sem.at[1, i], to_group, to_part,
            )
        )
        filter_grad_ref[channel] = send_filter_grad[i, part]
        through_ref[channel] = send_through[i, me]

    def held_by(i, b):
        return filter_grad_ref.at[pl.ds(i * devices + b * parts, parts)]

    for i in range(count):
        wait_bytes(
            filter_grad_ref.at[pl.ds(i * devices, parts - 1)], filter_grad_sem.at[1, i]
        )
        for lead in range(1, groups):
            remote(
                held_by(i, group), held_by(i, group), relay_sem.at[0, i], relay_sem.at[1, i],
                after(group, lead, groups), part,
            )

    wait_bytes(send_f.at[pl.ds(0, parts - 1)], f_sem.at[0])
    wait_bytes(send_gx.at[pl.ds(0, devices - 1)], gx_sem.at[0])
    for i in range(count):
        wait_bytes(send_filter_grad.at[i, pl.ds(0, parts - 1)], filter_grad_sem.at[0, i])
        for side in range(2):
            wait_bytes(send_through.at[i, pl.ds(0, devices - 1)], through_sem.at[side, i])
            relayed = pl.ds(i * devices, (groups - 1) * parts)
            wait_bytes(filter_grad_ref.at[relayed], relay_sem.at[side, i])


def fused_body(groups, parts, inputs, cotangent, filters, skip_gain):
    channels, width = filters.shape
    rows, half = width // LANES, parts * width // LANES
    devices = groups * parts
    count = channels // devices
    outer, phi, inner, back = dft_tables(parts * width)
    outer_high, outer_low = np_split(outer)
    tables = (
        np.concatenate([outer_high, outer_low], axis=1),
        np.concatenate([outer_high, outer_low, outer_high], axis=1),
        phi,
        np.stack(np_split(inner)),
        np.stack(np_split(inner.T)),
        np.stack(np_split(back)),
    )
    tables = tuple(jnp.asarray(t) for t in tables)
    operands = (inputs, cotangent, filters) + tables
    tile = (rows, LANES)
    whole = jax.ShapeDtypeStruct((channels,) + tile, jnp.float32)
    through, filter_grad = pl.pallas_call(
        functools.partial(kernel, groups, parts, count, half),
        out_shape=(whole, whole),
        in_specs=[pl.BlockSpec(memory_space=pltpu.HBM)] * len(operands),
        out_specs=(pl.BlockSpec(memory_space=pltpu.VMEM),) * 2,
        scratch_shapes=[pltpu.VMEM(t.shape, t.dtype) for t in operands] + [
            pltpu.VMEM((devices, count, 2) + tile, jnp.float32),
            pltpu.VMEM((devices, count) + tile, jnp.float32),
            pltpu.VMEM((devices, count, 2) + tile, jnp.float32),
            pltpu.VMEM((parts, count) + tile, jnp.float32),
            pltpu.VMEM((count, devices) + tile, jnp.float32),
            pltpu.VMEM((count, parts) + tile, jnp.float32),
            pltpu.SemaphoreType.DMA((len(operands),)),
        ] + [pltpu.SemaphoreType.DMA((2,))] * 2 + [pltpu.SemaphoreType.DMA((2, count))] * 3,
        compiler_params=pltpu.CompilerParams(collective_id=0, has_side_effects=True),
    )(*operands)
    through = through.reshape(channels, width)
    input_grad = through + skip_gain[:, None] * cotangent[0].astype(jnp.float32)
    return input_grad.astype(jnp.bfloat16)[None], filter_grad.reshape(channels, width)


def solution(mesh):
    groups, parts = mesh.shape["dp"], mesh.shape["ctx"]

    def body(inputs, cotangent, filters, skip_gain):
        if filters.shape[0] % (groups * parts) or inputs.shape[0] != 1:
            return plain_body(inputs, cotangent, filters, skip_gain)
        return fused_body(groups, parts, inputs, cotangent, filters, skip_gain)

    return jax.shard_map(
        body,
        mesh=mesh,
        in_specs=(P("dp", None, "ctx"), P("dp", None, "ctx"), P(None, "ctx"), P()),
        out_specs=(P("dp", None, "ctx"), P(None, "ctx")),
        check_vma=False,
    )
```

```python
import functools
import math

import jax
import jax.numpy as jnp
import ml_dtypes
import numpy as np
from jax import lax
from jax.experimental import pallas as pl
from jax.experimental.pallas import tpu as pltpu
from jax.sharding import PartitionSpec as P

LANES = 128
MESH = pl.DeviceIdType.MESH


def dft_tables(length):
    half = length // LANES
    row = np.arange(half)
    lane = np.arange(LANES)
    theta = 2 * math.pi / (2 * half) * (((row[:, None] + 0.5) * row[None, :]) % (2 * half))
    outer = np.concatenate([np.cos(theta), -np.sin(theta)])
    phi = math.pi / length * ((row[:, None] + 0.5) * lane[None, :])
    phi_table = np.stack([np.cos(phi), -np.sin(phi)])
    psi = 2 * math.pi / LANES * ((lane[:, None] * lane[None, :]) % LANES)
    cos, sin = np.cos(psi), np.sin(psi)
    inner = np.block([[cos, -sin], [sin, cos]])
    back = outer.T / length / math.sqrt(length)
    return outer, phi_table.astype(np.float32), inner, back


def np_split(table):
    high = table.astype(ml_dtypes.bfloat16)
    low = (table - high.astype(np.float64)).astype(ml_dtypes.bfloat16)
    return high, low


def split(values):
    high = values.astype(jnp.bfloat16)
    return high, (values - high.astype(jnp.float32)).astype(jnp.bfloat16)


def dot(left, right):
    return jnp.dot(left, right, preferred_element_type=jnp.float32)


def plain_gradients(grads, inputs, filters):
    batch, channels, length = grads.shape
    half = length // LANES
    outer, phi, inner, back = dft_tables(length)
    outer, inner, back = (t.astype(np.float32) for t in (outer, inner, back))
    product = functools.partial(jnp.matmul, precision=lax.Precision.HIGHEST)

    def forward(values):
        rows = product(outer, values.reshape(values.shape[:-1] + (half, LANES)))
        real, imag = rows[..., :half, :], rows[..., half:, :]
        turned = jnp.concatenate(
            [real * phi[0] - imag * phi[1], real * phi[1] + imag * phi[0]], axis=-1
        )
        spec = product(turned, inner)
        return spec[..., :LANES], spec[..., LANES:]

    def backward(real, imag):
        rows = product(jnp.concatenate([real, imag], axis=-1), inner.T)
        real, imag = rows[..., :LANES], rows[..., LANES:]
        turned = jnp.concatenate(
            [real * phi[0] + imag * phi[1], imag * phi[0] - real * phi[1]], axis=-2
        )
        out = product(back, turned)
        return out.reshape(out.shape[:-2] + (length,))

    def conj_product(first, second):
        return (
            first[0] * second[0] + first[1] * second[1],
            first[0] * second[1] - first[1] * second[0],
        )

    grad_spec = forward(grads)
    through = backward(*conj_product(forward(filters), grad_spec))
    real, imag = conj_product(forward(inputs), grad_spec)
    return through, backward(real.sum(0), imag.sum(0))


def plain_body(inputs, cotangent, filters, skip_gain):
    def gather(values):
        return lax.all_to_all(values, "ctx", 0, 1, tiled=True)

    grad_rows = cotangent[0].astype(jnp.float32)
    grads, rows = gather(grad_rows), gather(inputs[0].astype(jnp.float32))
    through, filter_grad = plain_gradients(grads[None], rows[None], gather(filters))
    filter_grad = lax.psum(filter_grad, "dp")
    through = lax.all_to_all(through[0], "ctx", 1, 0, tiled=True)
    filter_grad = lax.all_to_all(filter_grad, "ctx", 1, 0, tiled=True)
    return (through + skip_gain[:, None] * grad_rows).astype(jnp.bfloat16)[None], filter_grad


def kernel(
    groups, parts, count, half,
    x_hbm, g_hbm, f_hbm, outer_hbm, outer3_hbm, phi_hbm, inner_hbm, inner_t_hbm, back_hbm,
    through_ref, filter_grad_ref,
    x_ref, g_ref, f_ref, outer_ref, outer3_ref, phi_ref, inner_ref, inner_t_ref, back_ref,
    send_gx, send_f, recv_gx, recv_f, send_through, send_filter_grad,
    load_sem, gx_sem, f_sem, through_sem, filter_grad_sem, relay_sem,
):
    devices = groups * parts
    rows = x_ref.shape[2] // LANES
    group, part = lax.axis_index("dp"), lax.axis_index("ctx")
    me = group * parts + part

    loads = [
        pltpu.make_async_copy(source, target, load_sem.at[n])
        for n, (source, target) in enumerate(
            [
                (g_hbm, g_ref), (x_hbm, x_ref), (f_hbm, f_ref),
                (outer_hbm, outer_ref), (outer3_hbm, outer3_ref), (phi_hbm, phi_ref),
                (inner_hbm, inner_ref), (inner_t_hbm, inner_t_ref), (back_hbm, back_ref),
            ]
        )
    ]
    for load in loads:
        load.start()

    def after(position, step, size):
        moved = position + step
        return jnp.where(moved >= size, moved - size, moved)

    def each_other(act):
        for lead in range(groups):
            there = after(group, lead, groups)

            @pl.loop(0 if lead else 1, parts)
            def _(step):
                act(there, after(part, step, parts))

    barrier = pltpu.get_barrier_semaphore()
    each_other(
        lambda to_group, to_part: pl.semaphore_signal(
            barrier, inc=1, device_id=(to_group, to_part), device_id_type=MESH
        )
    )

    def remote(source, target, sems, i, to_group, to_part):
        pltpu.make_async_remote_copy(
            src_ref=source,
            dst_ref=target,
            send_sem=sems.at[0, i],
            recv_sem=sems.at[1, i],
            device_id=(to_group, to_part),
            device_id_type=MESH,
        ).start()

    def wait_bytes(held, sem):
        pltpu.make_async_copy(held, held, sem).wait()

    def pack(target, source):
        for r in range(rows):
            target[:, r, :] = source[:, r * LANES:(r + 1) * LANES].astype(jnp.float32)

    def send_filters(i):
        @pl.loop(1, parts)
        def _(step):
            other = after(part, step, parts)
            remote(
                send_f.at[i, group * parts + other], recv_f.at[i, part], f_sem, i, group, other
            )

        recv_f[i, part] = send_f[i, me]

    def send_rows(i, kind):
        each_other(
            lambda to_group, to_part: remote(
                send_gx.at[i, kind, to_group * parts + to_part], recv_gx.at[i, kind, me],
                gx_sem, 2 * i + kind, to_group, to_part,
            )
        )
        recv_gx[i, kind, me] = send_gx[i, kind, me]

    for i in range(count):
        own = slice(i * devices, (i + 1) * devices)
        for kind, source in enumerate((g_ref, x_ref)):
            if i == 0:
                loads[kind].wait()
            if kind == 0:
                if i == 0:
                    loads[2].wait()
                pack(send_f.at[i], f_ref.at[own])
            pack(send_gx.at[i, kind], source.at[0, own])
            if i == 0 and kind == 0:
                pl.semaphore_wait(barrier, devices - 1)
            if kind == 0:
                send_filters(i)
            send_rows(i, kind)
    for load in loads[3:]:
        load.wait()

    def turn(real, imag, sine):
        cosine = phi_ref[0]
        return real * cosine - imag * sine, real * sine + imag * cosine

    def along_lanes(pairs, table_ref):
        values = jnp.concatenate([jnp.concatenate(pair, axis=1) for pair in pairs], axis=0)
        high, low = split(values)
        out = dot(jnp.concatenate([high, low, high], axis=1), table_ref[...])
        blocks = [out[s * half:(s + 1) * half] for s in range(len(pairs))]
        return [(block[:, :LANES], block[:, LANES:]) for block in blocks]

    def forward(stepped):
        blocks = [stepped[:, s:s + LANES] for s in range(0, stepped.shape[1], LANES)]
        pairs = [turn(block[:half], block[half:], phi_ref[1]) for block in blocks]
        return along_lanes(pairs, inner_ref)

    def backward(specs):
        pairs = [turn(real, imag, -phi_ref[1]) for real, imag in along_lanes(specs, inner_t_ref)]
        values = jnp.concatenate([jnp.concatenate(pair, axis=0) for pair in pairs], axis=1)
        high, low = split(values)
        out = dot(back_ref[...], jnp.concatenate([high, high, low], axis=0))
        return [
            out[:, s:s + LANES].reshape(parts, rows, LANES) for s in range(0, out.shape[1], LANES)
        ]

    def conj_product(first, second):
        return (
            first[0] * second[0] + first[1] * second[1],
            first[0] * second[1] - first[1] * second[0],
        )

    def step_rows(i, kind):
        wait_bytes(recv_gx.at[i, kind, pl.ds(0, devices - 1)], gx_sem.at[1, 2 * i + kind])
        exact = jnp.concatenate(
            [
                recv_gx[i, kind, b * parts:(b + 1) * parts].reshape(half, LANES)
                for b in range(groups)
            ],
            axis=1,
        ).astype(jnp.bfloat16)
        return dot(outer_ref[...], jnp.concatenate([exact, exact], axis=0))

    def held_by(i, b):
        return filter_grad_ref.at[pl.ds(i * devices + b * parts, parts)]

    def relay(i):
        wait_bytes(
            filter_grad_ref.at[pl.ds(i * devices, parts - 1)], filter_grad_sem.at[1, i]
        )
        for lead in range(1, groups):
            remote(
                held_by(i, group), held_by(i, group), relay_sem, i, after(group, lead, groups), part
            )

    for i in range(count):
        channel = i * devices + me
        wait_bytes(recv_f.at[i, pl.ds(0, parts - 1)], f_sem.at[1, i])
        high, low = split(recv_f[i].reshape(half, LANES))
        filter_part = dot(outer3_ref[...], jnp.concatenate([high, high, low], axis=0))
        *grad_specs, filter_spec = forward(
            jnp.concatenate([step_rows(i, 0), filter_part], axis=1)
        )
        through = backward([conj_product(filter_spec, spec) for spec in grad_specs])
        for b in range(groups):
            send_through[i, b * parts:(b + 1) * parts] = through[b]
        each_other(
            lambda to_group, to_part: remote(
                send_through.at[i, to_group * parts + to_part], through_ref.at[channel],
                through_sem, i, to_group, to_part,
            )
        )
        through_ref[channel] = send_through[i, me]
        if i:
            relay(i - 1)

        terms = [
            conj_product(first, second)
            for first, second in zip(forward(step_rows(i, 1)), grad_specs)
        ]
        total = (sum(term[0] for term in terms), sum(term[1] for term in terms))
        send_filter_grad[i] = backward([total])[0]

        @pl.loop(1, parts)
        def _(step):
            other = after(part, step, parts)
            remote(
                send_filter_grad.at[i, other], filter_grad_ref.at[channel],
                filter_grad_sem, i, group, other,
            )

        filter_grad_ref[channel] = send_filter_grad[i, part]
    relay(count - 1)

    for i in range(count):
        wait_bytes(send_f.at[i, pl.ds(0, parts - 1)], f_sem.at[0, i])
        for kind in range(2):
            wait_bytes(send_gx.at[i, kind, pl.ds(0, devices - 1)], gx_sem.at[0, 2 * i + kind])
        wait_bytes(send_filter_grad.at[i, pl.ds(0, parts - 1)], filter_grad_sem.at[0, i])
        for side in range(2):
            wait_bytes(send_through.at[i, pl.ds(0, devices - 1)], through_sem.at[side, i])
            relayed = pl.ds(i * devices, (groups - 1) * parts)
            wait_bytes(filter_grad_ref.at[relayed], relay_sem.at[side, i])


def fused_body(groups, parts, inputs, cotangent, filters, skip_gain):
    channels, width = filters.shape
    rows, half = width // LANES, parts * width // LANES
    devices = groups * parts
    count = channels // devices
    outer, phi, inner, back = dft_tables(parts * width)
    outer_high, outer_low = np_split(outer)
    inner_high, inner_low = np_split(inner)
    back_high, back_low = np_split(back)
    tables = (
        np.concatenate([outer_high, outer_low], axis=1),
        np.concatenate([outer_high, outer_low, outer_high], axis=1),
        phi,
        np.concatenate([inner_high, inner_high, inner_low]),
        np.concatenate([inner_high.T, inner_high.T, inner_low.T]),
        np.concatenate([back_high, back_low, back_high], axis=1),
    )
    tables = tuple(jnp.asarray(t) for t in tables)
    operands = (inputs, cotangent, filters) + tables
    tile = (rows, LANES)
    whole = jax.ShapeDtypeStruct((channels,) + tile, jnp.float32)
    through, filter_grad = pl.pallas_call(
        functools.partial(kernel, groups, parts, count, half),
        out_shape=(whole, whole),
        in_specs=[pl.BlockSpec(memory_space=pltpu.HBM)] * len(operands),
        out_specs=(pl.BlockSpec(memory_space=pltpu.VMEM),) * 2,
        scratch_shapes=[pltpu.VMEM(t.shape, t.dtype) for t in operands] + [
            pltpu.VMEM((count, 2, devices) + tile, jnp.float32),
            pltpu.VMEM((count, devices) + tile, jnp.float32),
            pltpu.VMEM((count, 2, devices) + tile, jnp.float32),
            pltpu.VMEM((count, parts) + tile, jnp.float32),
            pltpu.VMEM((count, devices) + tile, jnp.float32),
            pltpu.VMEM((count, parts) + tile, jnp.float32),
            pltpu.SemaphoreType.DMA((len(operands),)),
        ] + [pltpu.SemaphoreType.DMA((2, 2 * count))] * 5,
        compiler_params=pltpu.CompilerParams(collective_id=0, has_side_effects=True),
    )(*operands)
    through = through.reshape(channels, width)
    input_grad = through + skip_gain[:, None] * cotangent[0].astype(jnp.float32)
    return input_grad.astype(jnp.bfloat16)[None], filter_grad.reshape(channels, width)


def solution(mesh):
    groups, parts = mesh.shape["dp"], mesh.shape["ctx"]

    def body(inputs, cotangent, filters, skip_gain):
        if filters.shape[0] % (groups * parts) or inputs.shape[0] != 1:
            return plain_body(inputs, cotangent, filters, skip_gain)
        return fused_body(groups, parts, inputs, cotangent, filters, skip_gain)

    return jax.shard_map(
        body,
        mesh=mesh,
        in_specs=(P("dp", None, "ctx"), P("dp", None, "ctx"), P(None, "ctx"), P()),
        out_specs=(P("dp", None, "ctx"), P(None, "ctx")),
        check_vma=False,
    )
```

```python
import functools
import math

import jax
import jax.numpy as jnp
import ml_dtypes
import numpy as np
from jax import lax
from jax.experimental import pallas as pl
from jax.experimental.pallas import tpu as pltpu
from jax.sharding import PartitionSpec as P

LANES = 128
MESH = pl.DeviceIdType.MESH


def dft_tables(length):
    half = length // LANES
    row = np.arange(half)
    lane = np.arange(LANES)
    theta = 2 * math.pi / (2 * half) * (((row[:, None] + 0.5) * row[None, :]) % (2 * half))
    outer = np.concatenate([np.cos(theta), -np.sin(theta)])
    phi = math.pi / length * ((row[:, None] + 0.5) * lane[None, :])
    phi_table = np.stack([np.cos(phi), -np.sin(phi)])
    psi = 2 * math.pi / LANES * ((lane[:, None] * lane[None, :]) % LANES)
    cos, sin = np.cos(psi), np.sin(psi)
    inner = np.block([[cos, -sin], [sin, cos]])
    back = outer.T / length / math.sqrt(length)
    return outer, phi_table.astype(np.float32), inner, back


def np_split(table):
    high = table.astype(ml_dtypes.bfloat16)
    low = (table - high.astype(np.float64)).astype(ml_dtypes.bfloat16)
    return high, low


def split(values):
    high = values.astype(jnp.bfloat16)
    return high, (values - high.astype(jnp.float32)).astype(jnp.bfloat16)


def dot(left, right):
    return jnp.dot(left, right, preferred_element_type=jnp.float32)


def plain_gradients(grads, inputs, filters):
    batch, channels, length = grads.shape
    half = length // LANES
    outer, phi, inner, back = dft_tables(length)
    outer, inner, back = (t.astype(np.float32) for t in (outer, inner, back))
    product = functools.partial(jnp.matmul, precision=lax.Precision.HIGHEST)

    def forward(values):
        rows = product(outer, values.reshape(values.shape[:-1] + (half, LANES)))
        real, imag = rows[..., :half, :], rows[..., half:, :]
        turned = jnp.concatenate(
            [real * phi[0] - imag * phi[1], real * phi[1] + imag * phi[0]], axis=-1
        )
        spec = product(turned, inner)
        return spec[..., :LANES], spec[..., LANES:]

    def backward(real, imag):
        rows = product(jnp.concatenate([real, imag], axis=-1), inner.T)
        real, imag = rows[..., :LANES], rows[..., LANES:]
        turned = jnp.concatenate(
            [real * phi[0] + imag * phi[1], imag * phi[0] - real * phi[1]], axis=-2
        )
        out = product(back, turned)
        return out.reshape(out.shape[:-2] + (length,))

    def conj_product(first, second):
        return (
            first[0] * second[0] + first[1] * second[1],
            first[0] * second[1] - first[1] * second[0],
        )

    grad_spec = forward(grads)
    through = backward(*conj_product(forward(filters), grad_spec))
    real, imag = conj_product(forward(inputs), grad_spec)
    return through, backward(real.sum(0), imag.sum(0))


def plain_body(inputs, cotangent, filters, skip_gain):
    def gather(values):
        return lax.all_to_all(values, "ctx", 0, 1, tiled=True)

    grad_rows = cotangent[0].astype(jnp.float32)
    grads, rows = gather(grad_rows), gather(inputs[0].astype(jnp.float32))
    through, filter_grad = plain_gradients(grads[None], rows[None], gather(filters))
    filter_grad = lax.psum(filter_grad, "dp")
    through = lax.all_to_all(through[0], "ctx", 1, 0, tiled=True)
    filter_grad = lax.all_to_all(filter_grad, "ctx", 1, 0, tiled=True)
    return (through + skip_gain[:, None] * grad_rows).astype(jnp.bfloat16)[None], filter_grad


def kernel(
    groups, parts, count, half,
    x_hbm, g_hbm, f_hbm, outer_hbm, outer3_hbm, phi_hbm, inner_hbm, inner_t_hbm, back_hbm,
    through_ref, filter_grad_ref,
    x_ref, g_ref, f_ref, outer_ref, outer3_ref, phi_ref, inner_ref, inner_t_ref, back_ref,
    send_gx, send_f, recv_gx, recv_f, send_through, send_filter_grad,
    load_sem, gx_sem, f_sem, through_sem, filter_grad_sem, relay_sem,
):
    devices = groups * parts
    rows = x_ref.shape[2] // LANES
    group, part = lax.axis_index("dp"), lax.axis_index("ctx")
    me = group * parts + part

    loads = [
        pltpu.make_async_copy(source, target, load_sem.at[n])
        for n, (source, target) in enumerate(
            [
                (g_hbm, g_ref), (x_hbm, x_ref), (f_hbm, f_ref),
                (outer_hbm, outer_ref), (outer3_hbm, outer3_ref), (phi_hbm, phi_ref),
                (inner_hbm, inner_ref), (inner_t_hbm, inner_t_ref), (back_hbm, back_ref),
            ]
        )
    ]
    for load in loads:
        load.start()

    def after(position, step, size):
        moved = position + step
        return jnp.where(moved >= size, moved - size, moved)

    others = [after(part, step, parts) for step in range(parts)]

    def each_other(act):
        for lead in range(groups):
            there = after(group, lead, groups)

            for step in range(0 if lead else 1, parts):
                act(there, others[step])

    barrier = pltpu.get_barrier_semaphore()
    each_other(
        lambda to_group, to_part: pl.semaphore_signal(
            barrier, inc=1, device_id=(to_group, to_part), device_id_type=MESH
        )
    )

    def remote(source, target, sems, i, to_group, to_part):
        pltpu.make_async_remote_copy(
            src_ref=source,
            dst_ref=target,
            send_sem=sems.at[0, i],
            recv_sem=sems.at[1, i],
            device_id=(to_group, to_part),
            device_id_type=MESH,
        ).start()

    def wait_bytes(held, sem):
        pltpu.make_async_copy(held, held, sem).wait()

    def pack(i):
        own = slice(i * devices, (i + 1) * devices)
        for r in range(rows):
            lanes = slice(r * LANES, (r + 1) * LANES)
            send_gx[i, :, 0, r, :] = g_ref[0, own, lanes].astype(jnp.float32)
            send_gx[i, :, 1, r, :] = x_ref[0, own, lanes].astype(jnp.float32)
            send_f[i, :, r, :] = f_ref[own, lanes]

    def send_rows(i):
        for other in others[1:]:
            remote(
                send_f.at[i, group * parts + other], recv_f.at[i, part], f_sem, i, group, other
            )

        each_other(
            lambda to_group, to_part: remote(
                send_gx.at[i, to_group * parts + to_part], recv_gx.at[i, me],
                gx_sem, i, to_group, to_part,
            )
        )
        recv_gx[i, me] = send_gx[i, me]
        recv_f[i, part] = send_f[i, me]

    for load in loads[:3]:
        load.wait()
    pack(0)
    pl.semaphore_wait(barrier, devices - 1)
    send_rows(0)
    for i in range(1, count):
        pack(i)
        send_rows(i)
    for load in loads[3:]:
        load.wait()

    def product3(left, right):
        (left_high, left_low), (right_high, right_low) = left, right
        return (
            dot(left_high, right_high) + dot(left_low, right_high) + dot(left_high, right_low)
        )

    def turn(real, imag, sine):
        cosine = phi_ref[0]
        return real * cosine - imag * sine, real * sine + imag * cosine

    for i in range(count):
        wait_bytes(recv_f.at[i, pl.ds(0, parts - 1)], f_sem.at[1, i])
        wait_bytes(recv_gx.at[i, pl.ds(0, devices - 1)], gx_sem.at[1, i])

        def signal(kind, b):
            return recv_gx[i, b * parts:(b + 1) * parts, kind].reshape(half, LANES).astype(jnp.bfloat16)

        exact = jnp.concatenate(
            [signal(0, b) for b in range(groups)] + [signal(1, b) for b in range(groups)], axis=1
        )
        high, low = split(recv_f[i].reshape(half, LANES))
        stepped = dot(outer_ref[...], jnp.concatenate([exact, exact], axis=0))
        filter_part = dot(outer3_ref[...], jnp.concatenate([high, high, low], axis=0))
        stepped = jnp.concatenate([stepped, filter_part], axis=1)
        turned = []
        for s in range(2 * groups + 1):
            lanes = slice(s * LANES, (s + 1) * LANES)
            pair = turn(stepped[:half, lanes], stepped[half:, lanes], phi_ref[1])
            turned.append(jnp.concatenate(pair, axis=1))
        spec = product3(split(jnp.concatenate(turned, axis=0)), (inner_ref[0], inner_ref[1]))

        def piece(s):
            block = spec[s * half:(s + 1) * half]
            return block[:, :LANES], block[:, LANES:]

        filter_spec = piece(2 * groups)
        products = []
        total = None
        for b in range(groups):
            grad_spec, input_spec = piece(b), piece(groups + b)
            for first in (filter_spec, input_spec):
                term = jnp.concatenate(
                    [
                        first[0] * grad_spec[0] + first[1] * grad_spec[1],
                        first[0] * grad_spec[1] - first[1] * grad_spec[0],
                    ],
                    axis=1,
                )
                if first is filter_spec:
                    products.append(term)
                else:
                    total = term if total is None else total + term
        products.append(total)
        folded = product3(split(jnp.concatenate(products, axis=0)), (inner_t_ref[0], inner_t_ref[1]))
        turned = []
        for s in range(groups + 1):
            block = folded[s * half:(s + 1) * half]
            pair = turn(block[:, :LANES], block[:, LANES:], -phi_ref[1])
            turned.append(jnp.concatenate(pair, axis=0))
        final = product3((back_ref[0], back_ref[1]), split(jnp.concatenate(turned, axis=1)))
        send_filter_grad[i] = final[:, groups * LANES:].reshape(parts, rows, LANES)
        for b in range(groups):
            through = final[:, b * LANES:(b + 1) * LANES]
            send_through[i, b * parts:(b + 1) * parts] = through.reshape(parts, rows, LANES)

        channel = i * devices + me

        for other in others[1:]:
            remote(
                send_filter_grad.at[i, other], filter_grad_ref.at[channel],
                filter_grad_sem, i, group, other,
            )

        each_other(
            lambda to_group, to_part: remote(
                send_through.at[i, to_group * parts + to_part], through_ref.at[channel],
                through_sem, i, to_group, to_part,
            )
        )
        filter_grad_ref[channel] = send_filter_grad[i, part]
        through_ref[channel] = send_through[i, me]

    def held_by(i, b):
        return filter_grad_ref.at[pl.ds(i * devices + b * parts, parts)]

    for i in range(count):
        wait_bytes(
            filter_grad_ref.at[pl.ds(i * devices, parts - 1)], filter_grad_sem.at[1, i]
        )
        for lead in range(1, groups):
            remote(
                held_by(i, group), held_by(i, group), relay_sem, i, after(group, lead, groups), part
            )

    for i in range(count):
        wait_bytes(send_f.at[i, pl.ds(0, parts - 1)], f_sem.at[0, i])
        wait_bytes(send_gx.at[i, pl.ds(0, devices - 1)], gx_sem.at[0, i])
        wait_bytes(send_filter_grad.at[i, pl.ds(0, parts - 1)], filter_grad_sem.at[0, i])
        for side in range(2):
            wait_bytes(send_through.at[i, pl.ds(0, devices - 1)], through_sem.at[side, i])
            relayed = pl.ds(i * devices, (groups - 1) * parts)
            wait_bytes(filter_grad_ref.at[relayed], relay_sem.at[side, i])


def fused_body(groups, parts, inputs, cotangent, filters, skip_gain):
    channels, width = filters.shape
    rows, half = width // LANES, parts * width // LANES
    devices = groups * parts
    count = channels // devices
    outer, phi, inner, back = dft_tables(parts * width)
    outer_high, outer_low = np_split(outer)
    tables = (
        np.concatenate([outer_high, outer_low], axis=1),
        np.concatenate([outer_high, outer_low, outer_high], axis=1),
        phi,
        np.stack(np_split(inner)),
        np.stack(np_split(inner.T)),
        np.stack(np_split(back)),
    )
    tables = tuple(jnp.asarray(t) for t in tables)
    operands = (inputs, cotangent, filters) + tables
    tile = (rows, LANES)
    whole = jax.ShapeDtypeStruct((channels,) + tile, jnp.float32)
    through, filter_grad = pl.pallas_call(
        functools.partial(kernel, groups, parts, count, half),
        out_shape=(whole, whole),
        in_specs=[pl.BlockSpec(memory_space=pltpu.HBM)] * len(operands),
        out_specs=(pl.BlockSpec(memory_space=pltpu.VMEM),) * 2,
        scratch_shapes=[pltpu.VMEM(t.shape, t.dtype) for t in operands] + [
            pltpu.VMEM((count, devices, 2) + tile, jnp.float32),
            pltpu.VMEM((count, devices) + tile, jnp.float32),
            pltpu.VMEM((count, devices, 2) + tile, jnp.float32),
            pltpu.VMEM((count, parts) + tile, jnp.float32),
            pltpu.VMEM((count, devices) + tile, jnp.float32),
            pltpu.VMEM((count, parts) + tile, jnp.float32),
            pltpu.SemaphoreType.DMA((len(operands),)),
        ] + [pltpu.SemaphoreType.DMA((2, count))] * 5,
        compiler_params=pltpu.CompilerParams(collective_id=0, has_side_effects=True),
    )(*operands)
    through = through.reshape(channels, width)
    input_grad = through + skip_gain[:, None] * cotangent[0].astype(jnp.float32)
    return input_grad.astype(jnp.bfloat16)[None], filter_grad.reshape(channels, width)


def solution(mesh):
    groups, parts = mesh.shape["dp"], mesh.shape["ctx"]

    def body(inputs, cotangent, filters, skip_gain):
        if filters.shape[0] % (groups * parts) or inputs.shape[0] != 1:
            return plain_body(inputs, cotangent, filters, skip_gain)
        return fused_body(groups, parts, inputs, cotangent, filters, skip_gain)

    return jax.shard_map(
        body,
        mesh=mesh,
        in_specs=(P("dp", None, "ctx"), P("dp", None, "ctx"), P(None, "ctx"), P()),
        out_specs=(P("dp", None, "ctx"), P(None, "ctx")),
        check_vma=False,
    )
```

```python
import functools
import math

import jax
import jax.numpy as jnp
import ml_dtypes
import numpy as np
from jax import lax
from jax.experimental import pallas as pl
from jax.experimental.pallas import tpu as pltpu
from jax.sharding import PartitionSpec as P

LANES = 128
MESH = pl.DeviceIdType.MESH


def dft_tables(length):
    half = length // LANES
    row = np.arange(half)
    lane = np.arange(LANES)
    theta = 2 * math.pi / (2 * half) * (((row[:, None] + 0.5) * row[None, :]) % (2 * half))
    outer = np.concatenate([np.cos(theta), -np.sin(theta)])
    phi = math.pi / length * ((row[:, None] + 0.5) * lane[None, :])
    phi_table = np.stack([np.cos(phi), -np.sin(phi)])
    psi = 2 * math.pi / LANES * ((lane[:, None] * lane[None, :]) % LANES)
    cos, sin = np.cos(psi), np.sin(psi)
    inner = np.block([[cos, -sin], [sin, cos]])
    back = outer.T / length / math.sqrt(length)
    return outer, phi_table.astype(np.float32), inner, back


def np_split(table):
    high = table.astype(ml_dtypes.bfloat16)
    low = (table - high.astype(np.float64)).astype(ml_dtypes.bfloat16)
    return high, low


def split(values):
    high = values.astype(jnp.bfloat16)
    return high, (values - high.astype(jnp.float32)).astype(jnp.bfloat16)


def dot(left, right):
    return jnp.dot(left, right, preferred_element_type=jnp.float32)


def plain_gradients(grads, inputs, filters):
    batch, channels, length = grads.shape
    half = length // LANES
    outer, phi, inner, back = dft_tables(length)
    outer, inner, back = (t.astype(np.float32) for t in (outer, inner, back))
    product = functools.partial(jnp.matmul, precision=lax.Precision.HIGHEST)

    def forward(values):
        rows = product(outer, values.reshape(values.shape[:-1] + (half, LANES)))
        real, imag = rows[..., :half, :], rows[..., half:, :]
        turned = jnp.concatenate(
            [real * phi[0] - imag * phi[1], real * phi[1] + imag * phi[0]], axis=-1
        )
        spec = product(turned, inner)
        return spec[..., :LANES], spec[..., LANES:]

    def backward(real, imag):
        rows = product(jnp.concatenate([real, imag], axis=-1), inner.T)
        real, imag = rows[..., :LANES], rows[..., LANES:]
        turned = jnp.concatenate(
            [real * phi[0] + imag * phi[1], imag * phi[0] - real * phi[1]], axis=-2
        )
        out = product(back, turned)
        return out.reshape(out.shape[:-2] + (length,))

    def conj_product(first, second):
        return (
            first[0] * second[0] + first[1] * second[1],
            first[0] * second[1] - first[1] * second[0],
        )

    grad_spec = forward(grads)
    through = backward(*conj_product(forward(filters), grad_spec))
    real, imag = conj_product(forward(inputs), grad_spec)
    return through, backward(real.sum(0), imag.sum(0))


def plain_body(inputs, cotangent, filters, skip_gain):
    def gather(values):
        return lax.all_to_all(values, "ctx", 0, 1, tiled=True)

    grad_rows = cotangent[0].astype(jnp.float32)
    grads, rows = gather(grad_rows), gather(inputs[0].astype(jnp.float32))
    through, filter_grad = plain_gradients(grads[None], rows[None], gather(filters))
    filter_grad = lax.psum(filter_grad, "dp")
    through = lax.all_to_all(through[0], "ctx", 1, 0, tiled=True)
    filter_grad = lax.all_to_all(filter_grad, "ctx", 1, 0, tiled=True)
    return (through + skip_gain[:, None] * grad_rows).astype(jnp.bfloat16)[None], filter_grad


def kernel(
    groups, parts, count, half,
    x_hbm, g_hbm, f_hbm, outer_hbm, outer3_hbm, phi_hbm, inner_hbm, inner_t_hbm, back_hbm,
    through_ref, filter_grad_ref,
    x_ref, g_ref, f_ref, outer_ref, outer3_ref, phi_ref, inner_ref, inner_t_ref, back_ref,
    send_gx, send_f, recv_gx, recv_f, send_grads, held_grads,
    load_sem, gx_sem, f_sem, grads_sem, through_sem, filter_grad_sem,
):
    devices = groups * parts
    rows = x_ref.shape[2] // LANES
    group, part = lax.axis_index("dp"), lax.axis_index("ctx")
    me = group * parts + part

    loads = [
        pltpu.make_async_copy(source, target, load_sem.at[n])
        for n, (source, target) in enumerate(
            [
                (g_hbm, g_ref), (x_hbm, x_ref), (f_hbm, f_ref),
                (outer_hbm, outer_ref), (outer3_hbm, outer3_ref), (phi_hbm, phi_ref),
                (inner_hbm, inner_ref), (inner_t_hbm, inner_t_ref), (back_hbm, back_ref),
            ]
        )
    ]
    for load in loads:
        load.start()

    def after(position, step, size):
        moved = position + step
        return jnp.where(moved >= size, moved - size, moved)

    others = [after(part, step, parts) for step in range(parts)]

    def each_other(act):
        for lead in range(groups):
            there = after(group, lead, groups)

            for step in range(0 if lead else 1, parts):
                act(there, others[step])

    barrier = pltpu.get_barrier_semaphore()
    each_other(
        lambda to_group, to_part: pl.semaphore_signal(
            barrier, inc=1, device_id=(to_group, to_part), device_id_type=MESH
        )
    )

    def remote(source, target, sems, i, to_group, to_part):
        pltpu.make_async_remote_copy(
            src_ref=source,
            dst_ref=target,
            send_sem=sems.at[0, i],
            recv_sem=sems.at[1, i],
            device_id=(to_group, to_part),
            device_id_type=MESH,
        ).start()

    def wait_bytes(held, sem):
        pltpu.make_async_copy(held, held, sem).wait()

    def pack(i):
        own = slice(i * devices, (i + 1) * devices)
        for r in range(rows):
            lanes = slice(r * LANES, (r + 1) * LANES)
            send_gx[i, :, 0, r, :] = g_ref[0, own, lanes].astype(jnp.float32)
            send_gx[i, :, 1, r, :] = x_ref[0, own, lanes].astype(jnp.float32)
            send_f[i, :, r, :] = f_ref[own, lanes]

    def send_rows(i):
        for other in others[1:]:
            remote(
                send_f.at[i, group * parts + other], recv_f.at[i, part], f_sem, i, group, other
            )

        each_other(
            lambda to_group, to_part: remote(
                send_gx.at[i, to_group * parts + to_part], recv_gx.at[i, me],
                gx_sem, i, to_group, to_part,
            )
        )
        recv_gx[i, me] = send_gx[i, me]
        recv_f[i, part] = send_f[i, me]

    for load in loads[:3]:
        load.wait()
    pack(0)
    pl.semaphore_wait(barrier, devices - 1)
    send_rows(0)
    for i in range(1, count):
        pack(i)
        send_rows(i)
    for load in loads[3:]:
        load.wait()

    def product3(left, right):
        (left_high, left_low), (right_high, right_low) = left, right
        return (
            dot(left_high, right_high) + dot(left_low, right_high) + dot(left_high, right_low)
        )

    def turn(real, imag, sine):
        cosine = phi_ref[0]
        return real * cosine - imag * sine, real * sine + imag * cosine

    for i in range(count):
        wait_bytes(recv_f.at[i, pl.ds(0, parts - 1)], f_sem.at[1, i])
        wait_bytes(recv_gx.at[i, pl.ds(0, devices - 1)], gx_sem.at[1, i])

        def signal(kind, b):
            return recv_gx[i, b * parts:(b + 1) * parts, kind].reshape(half, LANES).astype(jnp.bfloat16)

        exact = jnp.concatenate(
            [signal(0, b) for b in range(groups)] + [signal(1, b) for b in range(groups)], axis=1
        )
        high, low = split(recv_f[i].reshape(half, LANES))
        stepped = dot(outer_ref[...], jnp.concatenate([exact, exact], axis=0))
        filter_part = dot(outer3_ref[...], jnp.concatenate([high, high, low], axis=0))
        stepped = jnp.concatenate([stepped, filter_part], axis=1)
        turned = []
        for s in range(2 * groups + 1):
            lanes = slice(s * LANES, (s + 1) * LANES)
            pair = turn(stepped[:half, lanes], stepped[half:, lanes], phi_ref[1])
            turned.append(jnp.concatenate(pair, axis=1))
        spec = product3(split(jnp.concatenate(turned, axis=0)), (inner_ref[0], inner_ref[1]))

        def piece(s):
            block = spec[s * half:(s + 1) * half]
            return block[:, :LANES], block[:, LANES:]

        filter_spec = piece(2 * groups)
        products = []
        total = None
        for b in range(groups):
            grad_spec, input_spec = piece(b), piece(groups + b)
            for first in (filter_spec, input_spec):
                term = jnp.concatenate(
                    [
                        first[0] * grad_spec[0] + first[1] * grad_spec[1],
                        first[0] * grad_spec[1] - first[1] * grad_spec[0],
                    ],
                    axis=1,
                )
                if first is filter_spec:
                    products.append(term)
                else:
                    total = term if total is None else total + term
        products.append(total)
        folded = product3(split(jnp.concatenate(products, axis=0)), (inner_t_ref[0], inner_t_ref[1]))
        turned = []
        for s in range(groups + 1):
            block = folded[s * half:(s + 1) * half]
            pair = turn(block[:, :LANES], block[:, LANES:], -phi_ref[1])
            turned.append(jnp.concatenate(pair, axis=0))
        final = product3((back_ref[0], back_ref[1]), split(jnp.concatenate(turned, axis=1)))
        for b in range(groups + 1):
            gradient = final[:, b * LANES:(b + 1) * LANES]
            send_grads[i, :, b] = gradient.reshape(parts, rows, LANES)
        for other in others[1:]:
            remote(send_grads.at[i, other], held_grads.at[i, part], grads_sem, i, group, other)
        held_grads[i, part] = send_grads[i, part]

    for i in range(count):
        own = pl.ds(i * devices + group * parts, parts)
        wait_bytes(held_grads.at[i, pl.ds(0, parts - 1)], grads_sem.at[1, i])
        for lead in range(1, groups):
            there = after(group, lead, groups)
            remote(
                held_grads.at[i, pl.ds(0, parts), there], through_ref.at[own],
                through_sem, i, there, part,
            )
            remote(
                held_grads.at[i, pl.ds(0, parts), groups], filter_grad_ref.at[own],
                filter_grad_sem, i, there, part,
            )
        through_ref[own] = held_grads[i, :, group]
        filter_grad_ref[own] = held_grads[i, :, groups]

    for i in range(count):
        wait_bytes(send_f.at[i, pl.ds(0, parts - 1)], f_sem.at[0, i])
        wait_bytes(send_gx.at[i, pl.ds(0, devices - 1)], gx_sem.at[0, i])
        wait_bytes(send_grads.at[i, pl.ds(0, parts - 1)], grads_sem.at[0, i])
        others_rows = pl.ds(i * devices, (groups - 1) * parts)
        for side in range(2):
            wait_bytes(through_ref.at[others_rows], through_sem.at[side, i])
            wait_bytes(filter_grad_ref.at[others_rows], filter_grad_sem.at[side, i])


def fused_body(groups, parts, inputs, cotangent, filters, skip_gain):
    channels, width = filters.shape
    rows, half = width // LANES, parts * width // LANES
    devices = groups * parts
    count = channels // devices
    outer, phi, inner, back = dft_tables(parts * width)
    outer_high, outer_low = np_split(outer)
    tables = (
        np.concatenate([outer_high, outer_low], axis=1),
        np.concatenate([outer_high, outer_low, outer_high], axis=1),
        phi,
        np.stack(np_split(inner)),
        np.stack(np_split(inner.T)),
        np.stack(np_split(back)),
    )
    tables = tuple(jnp.asarray(t) for t in tables)
    operands = (inputs, cotangent, filters) + tables
    tile = (rows, LANES)
    whole = jax.ShapeDtypeStruct((channels,) + tile, jnp.float32)
    through, filter_grad = pl.pallas_call(
        functools.partial(kernel, groups, parts, count, half),
        out_shape=(whole, whole),
        in_specs=[pl.BlockSpec(memory_space=pltpu.HBM)] * len(operands),
        out_specs=(pl.BlockSpec(memory_space=pltpu.VMEM),) * 2,
        scratch_shapes=[pltpu.VMEM(t.shape, t.dtype) for t in operands] + [
            pltpu.VMEM((count, devices, 2) + tile, jnp.float32),
            pltpu.VMEM((count, devices) + tile, jnp.float32),
            pltpu.VMEM((count, devices, 2) + tile, jnp.float32),
            pltpu.VMEM((count, parts) + tile, jnp.float32),
            pltpu.VMEM((count, parts, groups + 1) + tile, jnp.float32),
            pltpu.VMEM((count, parts, groups + 1) + tile, jnp.float32),
            pltpu.SemaphoreType.DMA((len(operands),)),
        ] + [pltpu.SemaphoreType.DMA((2, count))] * 5,
        compiler_params=pltpu.CompilerParams(collective_id=0, has_side_effects=True),
    )(*operands)
    through = through.reshape(channels, width)
    input_grad = through + skip_gain[:, None] * cotangent[0].astype(jnp.float32)
    return input_grad.astype(jnp.bfloat16)[None], filter_grad.reshape(channels, width)


def solution(mesh):
    groups, parts = mesh.shape["dp"], mesh.shape["ctx"]

    def body(inputs, cotangent, filters, skip_gain):
        if filters.shape[0] % (groups * parts) or inputs.shape[0] != 1:
            return plain_body(inputs, cotangent, filters, skip_gain)
        return fused_body(groups, parts, inputs, cotangent, filters, skip_gain)

    return jax.shard_map(
        body,
        mesh=mesh,
        in_specs=(P("dp", None, "ctx"), P("dp", None, "ctx"), P(None, "ctx"), P()),
        out_specs=(P("dp", None, "ctx"), P(None, "ctx")),
        check_vma=False,
    )
```

```python
import functools
import math

import jax
import jax.numpy as jnp
import ml_dtypes
import numpy as np
from jax import lax
from jax.experimental import pallas as pl
from jax.experimental.pallas import tpu as pltpu
from jax.sharding import PartitionSpec as P

LANES = 128
MESH = pl.DeviceIdType.MESH


def dft_tables(length):
    half = length // LANES
    row = np.arange(half)
    lane = np.arange(LANES)
    theta = 2 * math.pi / (2 * half) * (((row[:, None] + 0.5) * row[None, :]) % (2 * half))
    outer = np.concatenate([np.cos(theta), -np.sin(theta)])
    phi = math.pi / length * ((row[:, None] + 0.5) * lane[None, :])
    phi_table = np.stack([np.cos(phi), -np.sin(phi)])
    psi = 2 * math.pi / LANES * ((lane[:, None] * lane[None, :]) % LANES)
    cos, sin = np.cos(psi), np.sin(psi)
    inner = np.block([[cos, -sin], [sin, cos]])
    back = outer.T / length / math.sqrt(length)
    return outer, phi_table.astype(np.float32), inner, back


def np_split(table):
    high = table.astype(ml_dtypes.bfloat16)
    low = (table - high.astype(np.float64)).astype(ml_dtypes.bfloat16)
    return high, low


def split(values):
    high = values.astype(jnp.bfloat16)
    return high, (values - high.astype(jnp.float32)).astype(jnp.bfloat16)


def dot(left, right):
    return jnp.dot(left, right, preferred_element_type=jnp.float32)


def plain_gradients(grads, inputs, filters):
    batch, channels, length = grads.shape
    half = length // LANES
    outer, phi, inner, back = dft_tables(length)
    outer, inner, back = (t.astype(np.float32) for t in (outer, inner, back))
    product = functools.partial(jnp.matmul, precision=lax.Precision.HIGHEST)

    def forward(values):
        rows = product(outer, values.reshape(values.shape[:-1] + (half, LANES)))
        real, imag = rows[..., :half, :], rows[..., half:, :]
        turned = jnp.concatenate(
            [real * phi[0] - imag * phi[1], real * phi[1] + imag * phi[0]], axis=-1
        )
        spec = product(turned, inner)
        return spec[..., :LANES], spec[..., LANES:]

    def backward(real, imag):
        rows = product(jnp.concatenate([real, imag], axis=-1), inner.T)
        real, imag = rows[..., :LANES], rows[..., LANES:]
        turned = jnp.concatenate(
            [real * phi[0] + imag * phi[1], imag * phi[0] - real * phi[1]], axis=-2
        )
        out = product(back, turned)
        return out.reshape(out.shape[:-2] + (length,))

    def conj_product(first, second):
        return (
            first[0] * second[0] + first[1] * second[1],
            first[0] * second[1] - first[1] * second[0],
        )

    grad_spec = forward(grads)
    through = backward(*conj_product(forward(filters), grad_spec))
    real, imag = conj_product(forward(inputs), grad_spec)
    return through, backward(real.sum(0), imag.sum(0))


def plain_body(inputs, cotangent, filters, skip_gain):
    def gather(values):
        return lax.all_to_all(values, "ctx", 0, 1, tiled=True)

    grad_rows = cotangent[0].astype(jnp.float32)
    grads, rows = gather(grad_rows), gather(inputs[0].astype(jnp.float32))
    through, filter_grad = plain_gradients(grads[None], rows[None], gather(filters))
    filter_grad = lax.psum(filter_grad, "dp")
    through = lax.all_to_all(through[0], "ctx", 1, 0, tiled=True)
    filter_grad = lax.all_to_all(filter_grad, "ctx", 1, 0, tiled=True)
    return (through + skip_gain[:, None] * grad_rows).astype(jnp.bfloat16)[None], filter_grad


def kernel(
    groups, parts, count, half,
    x_hbm, g_hbm, f_hbm, outer_hbm, outer3_hbm, phi_hbm, inner_hbm, inner_t_hbm, back_hbm,
    through_ref, filter_grad_ref,
    x_ref, g_ref, f_ref, outer_ref, outer3_ref, phi_ref, inner_ref, inner_t_ref, back_ref,
    send_gx, send_f, recv_gx, recv_f, send_through, send_filter_grad,
    load_sem, gx_sem, f_sem, through_sem, filter_grad_sem, relay_sem,
):
    devices = groups * parts
    rows = x_ref.shape[2] // LANES
    group, part = lax.axis_index("dp"), lax.axis_index("ctx")
    me = group * parts + part

    loads = [
        pltpu.make_async_copy(source, target, load_sem.at[n])
        for n, (source, target) in enumerate(
            [
                (g_hbm, g_ref), (x_hbm, x_ref), (f_hbm, f_ref),
                (outer_hbm, outer_ref), (outer3_hbm, outer3_ref), (phi_hbm, phi_ref),
                (inner_hbm, inner_ref), (inner_t_hbm, inner_t_ref), (back_hbm, back_ref),
            ]
        )
    ]
    for load in loads:
        load.start()

    def after(position, step, size):
        moved = position + step
        return jnp.where(moved >= size, moved - size, moved)

    others = [after(part, step, parts) for step in range(parts)]

    def each_other(act):
        for lead in range(groups):
            there = after(group, lead, groups)

            for step in range(0 if lead else 1, parts):
                act(there, others[step])

    barrier = pltpu.get_barrier_semaphore()
    each_other(
        lambda to_group, to_part: pl.semaphore_signal(
            barrier, inc=1, device_id=(to_group, to_part), device_id_type=MESH
        )
    )

    def remote(source, target, sems, to_group, to_part):
        pltpu.make_async_remote_copy(
            src_ref=source,
            dst_ref=target,
            send_sem=sems.at[0],
            recv_sem=sems.at[1],
            device_id=(to_group, to_part),
            device_id_type=MESH,
        ).start()

    def wait_bytes(held, sem):
        pltpu.make_async_copy(held, held, sem).wait()

    def pack(target, source):
        for i in range(count):
            for r in range(rows):
                block = source[i * devices:(i + 1) * devices, r * LANES:(r + 1) * LANES]
                target[:, i, r, :] = block.astype(jnp.float32)

    def send_rows(kind):
        each_other(
            lambda to_group, to_part: remote(
                send_gx.at[kind, to_group * parts + to_part], recv_gx.at[kind, me],
                gx_sem.at[kind], to_group, to_part,
            )
        )
        recv_gx[kind, me] = send_gx[kind, me]

    loads[2].wait()
    pack(send_f, f_ref)
    pl.semaphore_wait(barrier, devices - 1)
    for other in others[1:]:
        remote(send_f.at[group * parts + other], recv_f.at[part], f_sem, group, other)
    recv_f[part] = send_f[me]
    for kind, source in enumerate((g_ref, x_ref)):
        loads[kind].wait()
        pack(send_gx.at[kind], source.at[0])
        send_rows(kind)
    for load in loads[3:]:
        load.wait()

    def product3(left, right):
        (left_high, left_low), (right_high, right_low) = left, right
        return (
            dot(left_high, right_high) + dot(left_low, right_high) + dot(left_high, right_low)
        )

    def turn(real, imag, sine):
        cosine = phi_ref[0]
        return real * cosine - imag * sine, real * sine + imag * cosine

    def along_lanes(pairs, table_ref):
        rows_in = jnp.concatenate([jnp.concatenate(pair, axis=1) for pair in pairs], axis=0)
        out = product3(split(rows_in), (table_ref[0], table_ref[1]))
        blocks = [out[s * half:(s + 1) * half] for s in range(len(pairs))]
        return [(block[:, :LANES], block[:, LANES:]) for block in blocks]

    def forward(stepped):
        blocks = [stepped[:, s:s + LANES] for s in range(0, stepped.shape[1], LANES)]
        pairs = [turn(block[:half], block[half:], phi_ref[1]) for block in blocks]
        return along_lanes(pairs, inner_ref)

    def backward(specs):
        pairs = [turn(real, imag, -phi_ref[1]) for real, imag in along_lanes(specs, inner_t_ref)]
        turned = jnp.concatenate([jnp.concatenate(pair, axis=0) for pair in pairs], axis=1)
        out = product3((back_ref[0], back_ref[1]), split(turned))
        return [
            out[:, s:s + LANES].reshape(parts, rows, LANES) for s in range(0, out.shape[1], LANES)
        ]

    def conj_product(first, second):
        return (
            first[0] * second[0] + first[1] * second[1],
            first[0] * second[1] - first[1] * second[0],
        )

    def step_rows(kind):
        wait_bytes(recv_gx.at[kind, pl.ds(0, devices - 1)], gx_sem.at[kind, 1])
        exact = jnp.concatenate(
            [
                recv_gx[kind, b * parts:(b + 1) * parts, i].reshape(half, LANES)
                for i in range(count)
                for b in range(groups)
            ],
            axis=1,
        ).astype(jnp.bfloat16)
        return dot(outer_ref[...], jnp.concatenate([exact, exact], axis=0))

    both = pl.ds(0, count)
    wait_bytes(recv_f.at[pl.ds(0, parts - 1)], f_sem.at[1])
    high, low = split(
        jnp.concatenate([recv_f[:, i].reshape(half, LANES) for i in range(count)], axis=1)
    )
    filter_part = dot(outer3_ref[...], jnp.concatenate([high, high, low], axis=0))
    specs = forward(jnp.concatenate([step_rows(0), filter_part], axis=1))
    grad_specs, filter_specs = specs[:count * groups], specs[count * groups:]
    through = backward(
        [conj_product(filter_specs[s // groups], spec) for s, spec in enumerate(grad_specs)]
    )
    for s, tiles in enumerate(through):
        i, b = s // groups, s % groups
        send_through[b * parts:(b + 1) * parts, i] = tiles
    each_other(
        lambda to_group, to_part: remote(
            send_through.at[to_group * parts + to_part], through_ref.at[both, me],
            through_sem, to_group, to_part,
        )
    )
    through_ref[:, me] = send_through[me]

    terms = [
        conj_product(first, second) for first, second in zip(forward(step_rows(1)), grad_specs)
    ]
    totals = []
    for i in range(count):
        real, imag = zip(*terms[i * groups:(i + 1) * groups])
        totals.append((sum(real[1:], real[0]), sum(imag[1:], imag[0])))
    for i, tiles in enumerate(backward(totals)):
        send_filter_grad[:, i] = tiles
    for other in others[1:]:
        remote(
            send_filter_grad.at[other], filter_grad_ref.at[both, me], filter_grad_sem, group, other
        )
    filter_grad_ref[:, me] = send_filter_grad[part]

    own = filter_grad_ref.at[both, pl.ds(group * parts, parts)]
    wait_bytes(filter_grad_ref.at[both, pl.ds(0, parts - 1)], filter_grad_sem.at[1])
    for lead in range(1, groups):
        remote(own, own, relay_sem, after(group, lead, groups), part)

    wait_bytes(send_f.at[pl.ds(0, parts - 1)], f_sem.at[0])
    for kind in range(2):
        wait_bytes(send_gx.at[kind, pl.ds(0, devices - 1)], gx_sem.at[kind, 0])
    wait_bytes(send_filter_grad.at[pl.ds(0, parts - 1)], filter_grad_sem.at[0])
    for side in range(2):
        wait_bytes(send_through.at[pl.ds(0, devices - 1)], through_sem.at[side])
        wait_bytes(filter_grad_ref.at[both, pl.ds(0, (groups - 1) * parts)], relay_sem.at[side])


def fused_body(groups, parts, inputs, cotangent, filters, skip_gain):
    channels, width = filters.shape
    rows, half = width // LANES, parts * width // LANES
    devices = groups * parts
    count = channels // devices
    outer, phi, inner, back = dft_tables(parts * width)
    outer_high, outer_low = np_split(outer)
    tables = (
        np.concatenate([outer_high, outer_low], axis=1),
        np.concatenate([outer_high, outer_low, outer_high], axis=1),
        phi,
        np.stack(np_split(inner)),
        np.stack(np_split(inner.T)),
        np.stack(np_split(back)),
    )
    tables = tuple(jnp.asarray(t) for t in tables)
    operands = (inputs, cotangent, filters) + tables
    tile = (rows, LANES)
    whole = jax.ShapeDtypeStruct((count, devices) + tile, jnp.float32)
    through, filter_grad = pl.pallas_call(
        functools.partial(kernel, groups, parts, count, half),
        out_shape=(whole, whole),
        in_specs=[pl.BlockSpec(memory_space=pltpu.HBM)] * len(operands),
        out_specs=(pl.BlockSpec(memory_space=pltpu.VMEM),) * 2,
        scratch_shapes=[pltpu.VMEM(t.shape, t.dtype) for t in operands] + [
            pltpu.VMEM((2, devices, count) + tile, jnp.float32),
            pltpu.VMEM((devices, count) + tile, jnp.float32),
            pltpu.VMEM((2, devices, count) + tile, jnp.float32),
            pltpu.VMEM((parts, count) + tile, jnp.float32),
            pltpu.VMEM((devices, count) + tile, jnp.float32),
            pltpu.VMEM((parts, count) + tile, jnp.float32),
            pltpu.SemaphoreType.DMA((len(operands),)),
            pltpu.SemaphoreType.DMA((2, 2)),
        ] + [pltpu.SemaphoreType.DMA((2,))] * 4,
        compiler_params=pltpu.CompilerParams(collective_id=0, has_side_effects=True),
    )(*operands)
    through = through.reshape(channels, width)
    input_grad = through + skip_gain[:, None] * cotangent[0].astype(jnp.float32)
    return input_grad.astype(jnp.bfloat16)[None], filter_grad.reshape(channels, width)


def solution(mesh):
    groups, parts = mesh.shape["dp"], mesh.shape["ctx"]

    def body(inputs, cotangent, filters, skip_gain):
        if filters.shape[0] % (groups * parts) or inputs.shape[0] != 1:
            return plain_body(inputs, cotangent, filters, skip_gain)
        return fused_body(groups, parts, inputs, cotangent, filters, skip_gain)

    return jax.shard_map(
        body,
        mesh=mesh,
        in_specs=(P("dp", None, "ctx"), P("dp", None, "ctx"), P(None, "ctx"), P()),
        out_specs=(P("dp", None, "ctx"), P(None, "ctx")),
        check_vma=False,
    )
```

```python
import functools
import math

import jax
import jax.numpy as jnp
import ml_dtypes
import numpy as np
from jax import lax
from jax.experimental import pallas as pl
from jax.experimental.pallas import tpu as pltpu
from jax.sharding import PartitionSpec as P

LANES = 128
MESH = pl.DeviceIdType.MESH


def dft_tables(length):
    half = length // LANES
    row = np.arange(half)
    lane = np.arange(LANES)
    theta = 2 * math.pi / (2 * half) * (((row[:, None] + 0.5) * row[None, :]) % (2 * half))
    outer = np.concatenate([np.cos(theta), -np.sin(theta)])
    phi = math.pi / length * ((row[:, None] + 0.5) * lane[None, :])
    phi_table = np.stack([np.cos(phi), -np.sin(phi)])
    psi = 2 * math.pi / LANES * ((lane[:, None] * lane[None, :]) % LANES)
    cos, sin = np.cos(psi), np.sin(psi)
    inner = np.block([[cos, -sin], [sin, cos]])
    back = outer.T / length / math.sqrt(length)
    return outer, phi_table.astype(np.float32), inner, back


def np_split(table):
    high = table.astype(ml_dtypes.bfloat16)
    low = (table - high.astype(np.float64)).astype(ml_dtypes.bfloat16)
    return high, low


def split(values):
    high = values.astype(jnp.bfloat16)
    return high, (values - high.astype(jnp.float32)).astype(jnp.bfloat16)


def dot(left, right):
    return jnp.dot(left, right, preferred_element_type=jnp.float32)


def plain_gradients(grads, inputs, filters):
    batch, channels, length = grads.shape
    half = length // LANES
    outer, phi, inner, back = dft_tables(length)
    outer, inner, back = (t.astype(np.float32) for t in (outer, inner, back))
    product = functools.partial(jnp.matmul, precision=lax.Precision.HIGHEST)

    def forward(values):
        rows = product(outer, values.reshape(values.shape[:-1] + (half, LANES)))
        real, imag = rows[..., :half, :], rows[..., half:, :]
        turned = jnp.concatenate(
            [real * phi[0] - imag * phi[1], real * phi[1] + imag * phi[0]], axis=-1
        )
        spec = product(turned, inner)
        return spec[..., :LANES], spec[..., LANES:]

    def backward(real, imag):
        rows = product(jnp.concatenate([real, imag], axis=-1), inner.T)
        real, imag = rows[..., :LANES], rows[..., LANES:]
        turned = jnp.concatenate(
            [real * phi[0] + imag * phi[1], imag * phi[0] - real * phi[1]], axis=-2
        )
        out = product(back, turned)
        return out.reshape(out.shape[:-2] + (length,))

    def conj_product(first, second):
        return (
            first[0] * second[0] + first[1] * second[1],
            first[0] * second[1] - first[1] * second[0],
        )

    grad_spec = forward(grads)
    through = backward(*conj_product(forward(filters), grad_spec))
    real, imag = conj_product(forward(inputs), grad_spec)
    return through, backward(real.sum(0), imag.sum(0))


def plain_body(inputs, cotangent, filters, skip_gain):
    def gather(values):
        return lax.all_to_all(values, "ctx", 0, 1, tiled=True)

    grad_rows = cotangent[0].astype(jnp.float32)
    grads, rows = gather(grad_rows), gather(inputs[0].astype(jnp.float32))
    through, filter_grad = plain_gradients(grads[None], rows[None], gather(filters))
    filter_grad = lax.psum(filter_grad, "dp")
    through = lax.all_to_all(through[0], "ctx", 1, 0, tiled=True)
    filter_grad = lax.all_to_all(filter_grad, "ctx", 1, 0, tiled=True)
    return (through + skip_gain[:, None] * grad_rows).astype(jnp.bfloat16)[None], filter_grad


def kernel(
    groups, parts, count, half,
    x_hbm, g_hbm, f_hbm, outer_hbm, outer3_hbm, phi_hbm, inner_hbm, inner_t_hbm, back_hbm,
    skip_hbm,
    input_grad_ref, filter_grad_ref,
    x_ref, g_ref, f_ref, outer_ref, outer3_ref, phi_ref, inner_ref, inner_t_ref, back_ref,
    skip_ref,
    send_gx, send_f, recv_gx, recv_f, send_through, send_filter_grad,
    through_got, filter_grad_got,
    load_sem, gx_sem, f_sem, through_sem, filter_grad_sem, relay_sem,
):
    devices = groups * parts
    rows = x_ref.shape[2] // LANES
    group, part = lax.axis_index("dp"), lax.axis_index("ctx")
    me = group * parts + part

    loads = [
        pltpu.make_async_copy(source, target, load_sem.at[n])
        for n, (source, target) in enumerate(
            [
                (g_hbm, g_ref), (x_hbm, x_ref), (f_hbm, f_ref),
                (outer_hbm, outer_ref), (outer3_hbm, outer3_ref), (phi_hbm, phi_ref),
                (inner_hbm, inner_ref), (inner_t_hbm, inner_t_ref), (back_hbm, back_ref),
                (skip_hbm, skip_ref),
            ]
        )
    ]
    for load in loads:
        load.start()

    def after(position, step, size):
        moved = position + step
        return jnp.where(moved >= size, moved - size, moved)

    others = [after(part, step, parts) for step in range(parts)]

    def each_other(act):
        for lead in range(groups):
            there = after(group, lead, groups)

            for step in range(0 if lead else 1, parts):
                act(there, others[step])

    barrier = pltpu.get_barrier_semaphore()
    each_other(
        lambda to_group, to_part: pl.semaphore_signal(
            barrier, inc=1, device_id=(to_group, to_part), device_id_type=MESH
        )
    )

    def remote(source, target, sems, i, to_group, to_part):
        pltpu.make_async_remote_copy(
            src_ref=source,
            dst_ref=target,
            send_sem=sems.at[0, i],
            recv_sem=sems.at[1, i],
            device_id=(to_group, to_part),
            device_id_type=MESH,
        ).start()

    def wait_bytes(held, sem):
        pltpu.make_async_copy(held, held, sem).wait()

    def pack(i):
        own = slice(i * devices, (i + 1) * devices)
        for r in range(rows):
            lanes = slice(r * LANES, (r + 1) * LANES)
            send_gx[i, :, 0, r, :] = g_ref[0, own, lanes].astype(jnp.float32)
            send_gx[i, :, 1, r, :] = x_ref[0, own, lanes].astype(jnp.float32)
            send_f[i, :, r, :] = f_ref[own, lanes]

    def send_rows(i):
        for other in others[1:]:
            remote(
                send_f.at[i, group * parts + other], recv_f.at[i, part], f_sem, i, group, other
            )

        each_other(
            lambda to_group, to_part: remote(
                send_gx.at[i, to_group * parts + to_part], recv_gx.at[i, me],
                gx_sem, i, to_group, to_part,
            )
        )
        recv_gx[i, me] = send_gx[i, me]
        recv_f[i, part] = send_f[i, me]

    for load in loads[:3]:
        load.wait()
    pack(0)
    pl.semaphore_wait(barrier, devices - 1)
    send_rows(0)
    for i in range(1, count):
        pack(i)
        send_rows(i)
    for load in loads[3:]:
        load.wait()

    def product3(left, right):
        (left_high, left_low), (right_high, right_low) = left, right
        return (
            dot(left_high, right_high) + dot(left_low, right_high) + dot(left_high, right_low)
        )

    def turn(real, imag, sine):
        cosine = phi_ref[0]
        return real * cosine - imag * sine, real * sine + imag * cosine

    for i in range(count):
        wait_bytes(recv_f.at[i, pl.ds(0, parts - 1)], f_sem.at[1, i])
        wait_bytes(recv_gx.at[i, pl.ds(0, devices - 1)], gx_sem.at[1, i])

        def signal(kind, b):
            return recv_gx[i, b * parts:(b + 1) * parts, kind].reshape(half, LANES).astype(jnp.bfloat16)

        exact = jnp.concatenate(
            [signal(0, b) for b in range(groups)] + [signal(1, b) for b in range(groups)], axis=1
        )
        def forward(stepped):
            blocks = [stepped[:, k:k + LANES] for k in range(0, stepped.shape[1], LANES)]
            turned = [
                jnp.concatenate(turn(block[:half], block[half:], phi_ref[1]), axis=1)
                for block in blocks
            ]
            return pieces(jnp.concatenate(turned, axis=0), inner_ref)

        def pieces(values, table_ref):
            out = product3(split(values), (table_ref[0], table_ref[1]))
            blocks = [out[k:k + half] for k in range(0, out.shape[0], half)]
            return [(block[:, :LANES], block[:, LANES:]) for block in blocks]

        def backward(specs):
            values = jnp.concatenate([jnp.concatenate(pair, axis=1) for pair in specs], axis=0)
            turned = [
                jnp.concatenate(turn(real, imag, -phi_ref[1]), axis=0)
                for real, imag in pieces(values, inner_t_ref)
            ]
            out = product3((back_ref[0], back_ref[1]), split(jnp.concatenate(turned, axis=1)))
            blocks = [out[:, k:k + LANES] for k in range(0, out.shape[1], LANES)]
            return [block.reshape(parts, rows, LANES) for block in blocks]

        def conj_product(first, second):
            return (
                first[0] * second[0] + first[1] * second[1],
                first[0] * second[1] - first[1] * second[0],
            )

        exact = jnp.concatenate(
            [signal(0, b) for b in range(groups)] + [signal(1, b) for b in range(groups)], axis=1
        )
        specs = forward(dot(outer_ref[...], jnp.concatenate([exact, exact], axis=0)))
        grad_specs, input_specs = specs[:groups], specs[groups:]
        terms = [conj_product(first, second) for first, second in zip(input_specs, grad_specs)]
        real, imag = zip(*terms)
        send_filter_grad[i] = backward([(sum(real[1:], real[0]), sum(imag[1:], imag[0]))])[0]
        channel = i * devices + me
        for other in others[1:]:
            remote(
                send_filter_grad.at[i, other], filter_grad_got.at[channel],
                filter_grad_sem, i, group, other,
            )
        filter_grad_got[channel] = send_filter_grad[i, part]

        high, low = split(recv_f[i].reshape(half, LANES))
        filter_part = dot(outer3_ref[...], jnp.concatenate([high, high, low], axis=0))
        filter_spec = forward(filter_part)[0]
        for b, tiles in enumerate(backward([conj_product(filter_spec, g) for g in grad_specs])):
            send_through[i, b * parts:(b + 1) * parts] = tiles
        each_other(
            lambda to_group, to_part: remote(
                send_through.at[i, to_group * parts + to_part], through_got.at[channel],
                through_sem, i, to_group, to_part,
            )
        )
        through_got[channel] = send_through[i, me]

    def held_by(i, b):
        return filter_grad_got.at[pl.ds(i * devices + b * parts, parts)]

    for i in range(count):
        wait_bytes(
            filter_grad_got.at[pl.ds(i * devices, parts - 1)], filter_grad_sem.at[1, i]
        )
        for lead in range(1, groups):
            remote(
                held_by(i, group), held_by(i, group), relay_sem, i, after(group, lead, groups), part
            )

    size = skip_ref.shape[1]
    square = (size, size)
    on_diagonal = (
        lax.broadcasted_iota(jnp.int32, square, 0) == lax.broadcasted_iota(jnp.int32, square, 1)
    )
    skip = jnp.sum(jnp.where(on_diagonal, skip_ref[...], 0.0), axis=1, keepdims=True)
    for i in range(count):
        own = slice(i * devices, (i + 1) * devices)
        wait_bytes(send_through.at[i, pl.ds(0, devices - 1)], through_sem.at[1, i])
        for r in range(rows):
            lanes = slice(r * LANES, (r + 1) * LANES)
            skipped = skip[own] * g_ref[0, own, lanes].astype(jnp.float32)
            input_grad_ref[0, own, lanes] = (through_got[own, r, :] + skipped).astype(jnp.bfloat16)
        wait_bytes(filter_grad_got.at[pl.ds(0, (groups - 1) * parts)], relay_sem.at[1, i])
        for r in range(rows):
            filter_grad_ref[own, r * LANES:(r + 1) * LANES] = filter_grad_got[own, r, :]

    for i in range(count):
        wait_bytes(send_f.at[i, pl.ds(0, parts - 1)], f_sem.at[0, i])
        wait_bytes(send_gx.at[i, pl.ds(0, devices - 1)], gx_sem.at[0, i])
        wait_bytes(send_filter_grad.at[i, pl.ds(0, parts - 1)], filter_grad_sem.at[0, i])
        wait_bytes(send_through.at[i, pl.ds(0, devices - 1)], through_sem.at[0, i])
        wait_bytes(filter_grad_got.at[pl.ds(0, (groups - 1) * parts)], relay_sem.at[0, i])


def fused_body(groups, parts, inputs, cotangent, filters, skip_gain):
    channels, width = filters.shape
    rows, half = width // LANES, parts * width // LANES
    devices = groups * parts
    count = channels // devices
    outer, phi, inner, back = dft_tables(parts * width)
    outer_high, outer_low = np_split(outer)
    tables = (
        np.concatenate([outer_high, outer_low], axis=1),
        np.concatenate([outer_high, outer_low, outer_high], axis=1),
        phi,
        np.stack(np_split(inner)),
        np.stack(np_split(inner.T)),
        np.stack(np_split(back)),
    )
    tables = tuple(jnp.asarray(t) for t in tables)
    operands = (inputs, cotangent, filters) + tables + (skip_gain.reshape(1, channels),)
    tile = (rows, LANES)
    return pl.pallas_call(
        functools.partial(kernel, groups, parts, count, half),
        out_shape=(
            jax.ShapeDtypeStruct(cotangent.shape, jnp.bfloat16),
            jax.ShapeDtypeStruct(filters.shape, jnp.float32),
        ),
        in_specs=[pl.BlockSpec(memory_space=pltpu.HBM)] * len(operands),
        out_specs=(pl.BlockSpec(memory_space=pltpu.VMEM),) * 2,
        scratch_shapes=[pltpu.VMEM(t.shape, t.dtype) for t in operands] + [
            pltpu.VMEM((count, devices, 2) + tile, jnp.float32),
            pltpu.VMEM((count, devices) + tile, jnp.float32),
            pltpu.VMEM((count, devices, 2) + tile, jnp.float32),
            pltpu.VMEM((count, parts) + tile, jnp.float32),
            pltpu.VMEM((count, devices) + tile, jnp.float32),
            pltpu.VMEM((count, parts) + tile, jnp.float32),
            pltpu.VMEM((channels,) + tile, jnp.float32),
            pltpu.VMEM((channels,) + tile, jnp.float32),
            pltpu.SemaphoreType.DMA((len(operands),)),
        ] + [pltpu.SemaphoreType.DMA((2, count))] * 5,
        compiler_params=pltpu.CompilerParams(collective_id=0, has_side_effects=True),
    )(*operands)


def solution(mesh):
    groups, parts = mesh.shape["dp"], mesh.shape["ctx"]

    def body(inputs, cotangent, filters, skip_gain):
        if filters.shape[0] % (groups * parts) or inputs.shape[0] != 1:
            return plain_body(inputs, cotangent, filters, skip_gain)
        return fused_body(groups, parts, inputs, cotangent, filters, skip_gain)

    return jax.shard_map(
        body,
        mesh=mesh,
        in_specs=(P("dp", None, "ctx"), P("dp", None, "ctx"), P(None, "ctx"), P()),
        out_specs=(P("dp", None, "ctx"), P(None, "ctx")),
        check_vma=False,
    )
```

```python
import functools
import math

import jax
import jax.numpy as jnp
import ml_dtypes
import numpy as np
from jax import lax
from jax.experimental import pallas as pl
from jax.experimental.pallas import tpu as pltpu
from jax.sharding import PartitionSpec as P

LANES = 128
MESH = pl.DeviceIdType.MESH


def dft_tables(length):
    half = length // LANES
    row = np.arange(half)
    lane = np.arange(LANES)
    theta = 2 * math.pi / (2 * half) * (((row[:, None] + 0.5) * row[None, :]) % (2 * half))
    outer = np.concatenate([np.cos(theta), -np.sin(theta)])
    phi = math.pi / length * ((row[:, None] + 0.5) * lane[None, :])
    phi_table = np.stack([np.cos(phi), -np.sin(phi)])
    psi = 2 * math.pi / LANES * ((lane[:, None] * lane[None, :]) % LANES)
    cos, sin = np.cos(psi), np.sin(psi)
    inner = np.block([[cos, -sin], [sin, cos]])
    back = outer.T / length / math.sqrt(length)
    return outer, phi_table.astype(np.float32), inner, back


def np_split(table):
    high = table.astype(ml_dtypes.bfloat16)
    low = (table - high.astype(np.float64)).astype(ml_dtypes.bfloat16)
    return high, low


def split(values):
    high = values.astype(jnp.bfloat16)
    return high, (values - high.astype(jnp.float32)).astype(jnp.bfloat16)


def dot(left, right):
    return jnp.dot(left, right, preferred_element_type=jnp.float32)


def plain_gradients(grads, inputs, filters):
    batch, channels, length = grads.shape
    half = length // LANES
    outer, phi, inner, back = dft_tables(length)
    outer, inner, back = (t.astype(np.float32) for t in (outer, inner, back))
    product = functools.partial(jnp.matmul, precision=lax.Precision.HIGHEST)

    def forward(values):
        rows = product(outer, values.reshape(values.shape[:-1] + (half, LANES)))
        real, imag = rows[..., :half, :], rows[..., half:, :]
        turned = jnp.concatenate(
            [real * phi[0] - imag * phi[1], real * phi[1] + imag * phi[0]], axis=-1
        )
        spec = product(turned, inner)
        return spec[..., :LANES], spec[..., LANES:]

    def backward(real, imag):
        rows = product(jnp.concatenate([real, imag], axis=-1), inner.T)
        real, imag = rows[..., :LANES], rows[..., LANES:]
        turned = jnp.concatenate(
            [real * phi[0] + imag * phi[1], imag * phi[0] - real * phi[1]], axis=-2
        )
        out = product(back, turned)
        return out.reshape(out.shape[:-2] + (length,))

    def conj_product(first, second):
        return (
            first[0] * second[0] + first[1] * second[1],
            first[0] * second[1] - first[1] * second[0],
        )

    grad_spec = forward(grads)
    through = backward(*conj_product(forward(filters), grad_spec))
    real, imag = conj_product(forward(inputs), grad_spec)
    return through, backward(real.sum(0), imag.sum(0))


def plain_body(inputs, cotangent, filters, skip_gain):
    def gather(values):
        return lax.all_to_all(values, "ctx", 0, 1, tiled=True)

    grad_rows = cotangent[0].astype(jnp.float32)
    grads, rows = gather(grad_rows), gather(inputs[0].astype(jnp.float32))
    through, filter_grad = plain_gradients(grads[None], rows[None], gather(filters))
    filter_grad = lax.psum(filter_grad, "dp")
    through = lax.all_to_all(through[0], "ctx", 1, 0, tiled=True)
    filter_grad = lax.all_to_all(filter_grad, "ctx", 1, 0, tiled=True)
    return (through + skip_gain[:, None] * grad_rows).astype(jnp.bfloat16)[None], filter_grad


def kernel(
    groups, parts, count, half,
    x_hbm, g_hbm, f_hbm, outer_hbm, outer3_hbm, phi_hbm, inner_hbm, inner_t_hbm, back_hbm,
    skip_hbm,
    input_grad_ref, filter_grad_ref,
    x_ref, g_ref, f_ref, outer_ref, outer3_ref, phi_ref, inner_ref, inner_t_ref, back_ref,
    skip_ref,
    send_gx, send_f, recv_gx, recv_f, send_through, send_filter_grad,
    through_got, filter_grad_got,
    load_sem, gx_sem, f_sem, through_sem, filter_grad_sem, relay_sem,
):
    devices = groups * parts
    rows = x_ref.shape[2] // LANES
    group, part = lax.axis_index("dp"), lax.axis_index("ctx")
    me = group * parts + part

    loads = [
        pltpu.make_async_copy(source, target, load_sem.at[n])
        for n, (source, target) in enumerate(
            [
                (g_hbm, g_ref), (x_hbm, x_ref), (f_hbm, f_ref),
                (outer_hbm, outer_ref), (outer3_hbm, outer3_ref), (phi_hbm, phi_ref),
                (inner_hbm, inner_ref), (inner_t_hbm, inner_t_ref), (back_hbm, back_ref),
                (skip_hbm, skip_ref),
            ]
        )
    ]
    for load in loads:
        load.start()

    def after(position, step, size):
        moved = position + step
        return jnp.where(moved >= size, moved - size, moved)

    steps = sorted(range(parts), key=lambda step: abs(step - parts // 2))
    others = [after(part, step, parts) for step in steps if step]
    leads = [after(group, lead, groups) for lead in range(groups)]

    def each_other(act):
        for step in steps:
            for lead in range(0 if step else 1, groups):
                act(leads[lead], after(part, step, parts))

    barrier = pltpu.get_barrier_semaphore()
    each_other(
        lambda to_group, to_part: pl.semaphore_signal(
            barrier, inc=1, device_id=(to_group, to_part), device_id_type=MESH
        )
    )

    def remote(source, target, sems, i, to_group, to_part):
        pltpu.make_async_remote_copy(
            src_ref=source,
            dst_ref=target,
            send_sem=sems.at[0, i],
            recv_sem=sems.at[1, i],
            device_id=(to_group, to_part),
            device_id_type=MESH,
        ).start()

    def wait_bytes(held, sem):
        pltpu.make_async_copy(held, held, sem).wait()

    def pack(i):
        own = slice(i * devices, (i + 1) * devices)
        for r in range(rows):
            lanes = slice(r * LANES, (r + 1) * LANES)
            send_gx[i, :, 0, r, :] = g_ref[0, own, lanes].astype(jnp.float32)
            send_gx[i, :, 1, r, :] = x_ref[0, own, lanes].astype(jnp.float32)
            send_f[i, :, r, :] = f_ref[own, lanes]

    def send_rows(i):
        for other in others:
            remote(
                send_f.at[i, group * parts + other], recv_f.at[i, part], f_sem, i, group, other
            )

        each_other(
            lambda to_group, to_part: remote(
                send_gx.at[i, to_group * parts + to_part], recv_gx.at[i, me],
                gx_sem, i, to_group, to_part,
            )
        )
        recv_gx[i, me] = send_gx[i, me]
        recv_f[i, part] = send_f[i, me]

    for load in loads[:3]:
        load.wait()
    pack(0)
    pl.semaphore_wait(barrier, devices - 1)
    send_rows(0)
    for i in range(1, count):
        pack(i)
        send_rows(i)
    for load in loads[3:]:
        load.wait()

    def product3(left, right):
        (left_high, left_low), (right_high, right_low) = left, right
        return (
            dot(left_high, right_high) + dot(left_low, right_high) + dot(left_high, right_low)
        )

    def turn(real, imag, sine):
        cosine = phi_ref[0]
        return real * cosine - imag * sine, real * sine + imag * cosine

    for i in range(count):
        wait_bytes(recv_f.at[i, pl.ds(0, parts - 1)], f_sem.at[1, i])
        wait_bytes(recv_gx.at[i, pl.ds(0, devices - 1)], gx_sem.at[1, i])

        def signal(kind, b):
            return recv_gx[i, b * parts:(b + 1) * parts, kind].reshape(half, LANES).astype(jnp.bfloat16)

        exact = jnp.concatenate(
            [signal(0, b) for b in range(groups)] + [signal(1, b) for b in range(groups)], axis=1
        )
        def forward(stepped):
            blocks = [stepped[:, k:k + LANES] for k in range(0, stepped.shape[1], LANES)]
            turned = [
                jnp.concatenate(turn(block[:half], block[half:], phi_ref[1]), axis=1)
                for block in blocks
            ]
            return pieces(jnp.concatenate(turned, axis=0), inner_ref)

        def pieces(values, table_ref):
            out = product3(split(values), (table_ref[0], table_ref[1]))
            blocks = [out[k:k + half] for k in range(0, out.shape[0], half)]
            return [(block[:, :LANES], block[:, LANES:]) for block in blocks]

        def backward(specs):
            values = jnp.concatenate([jnp.concatenate(pair, axis=1) for pair in specs], axis=0)
            turned = [
                jnp.concatenate(turn(real, imag, -phi_ref[1]), axis=0)
                for real, imag in pieces(values, inner_t_ref)
            ]
            out = product3((back_ref[0], back_ref[1]), split(jnp.concatenate(turned, axis=1)))
            blocks = [out[:, k:k + LANES] for k in range(0, out.shape[1], LANES)]
            return [block.reshape(parts, rows, LANES) for block in blocks]

        def conj_product(first, second):
            return (
                first[0] * second[0] + first[1] * second[1],
                first[0] * second[1] - first[1] * second[0],
            )

        exact = jnp.concatenate(
            [signal(0, b) for b in range(groups)] + [signal(1, b) for b in range(groups)], axis=1
        )
        specs = forward(dot(outer_ref[...], jnp.concatenate([exact, exact], axis=0)))
        grad_specs, input_specs = specs[:groups], specs[groups:]
        terms = [conj_product(first, second) for first, second in zip(input_specs, grad_specs)]
        real, imag = zip(*terms)
        send_filter_grad[i] = backward([(sum(real[1:], real[0]), sum(imag[1:], imag[0]))])[0]
        channel = i * devices + me
        for other in others:
            remote(
                send_filter_grad.at[i, other], filter_grad_got.at[channel],
                filter_grad_sem, i, group, other,
            )
        filter_grad_got[channel] = send_filter_grad[i, part]

        high, low = split(recv_f[i].reshape(half, LANES))
        filter_part = dot(outer3_ref[...], jnp.concatenate([high, high, low], axis=0))
        filter_spec = forward(filter_part)[0]
        for b, tiles in enumerate(backward([conj_product(filter_spec, g) for g in grad_specs])):
            send_through[i, b * parts:(b + 1) * parts] = tiles
        each_other(
            lambda to_group, to_part: remote(
                send_through.at[i, to_group * parts + to_part], through_got.at[channel],
                through_sem, i, to_group, to_part,
            )
        )
        through_got[channel] = send_through[i, me]

    def held_by(i, b):
        return filter_grad_got.at[pl.ds(i * devices + b * parts, parts)]

    for i in range(count):
        wait_bytes(
            filter_grad_got.at[pl.ds(i * devices, parts - 1)], filter_grad_sem.at[1, i]
        )
        for lead in range(1, groups):
            remote(
                held_by(i, group), held_by(i, group), relay_sem, i, after(group, lead, groups), part
            )

    size = skip_ref.shape[1]
    square = (size, size)
    on_diagonal = (
        lax.broadcasted_iota(jnp.int32, square, 0) == lax.broadcasted_iota(jnp.int32, square, 1)
    )
    skip = jnp.sum(jnp.where(on_diagonal, skip_ref[...], 0.0), axis=1, keepdims=True)
    for i in range(count):
        own = slice(i * devices, (i + 1) * devices)
        wait_bytes(send_through.at[i, pl.ds(0, devices - 1)], through_sem.at[1, i])
        for r in range(rows):
            lanes = slice(r * LANES, (r + 1) * LANES)
            skipped = skip[own] * g_ref[0, own, lanes].astype(jnp.float32)
            input_grad_ref[0, own, lanes] = (through_got[own, r, :] + skipped).astype(jnp.bfloat16)
        wait_bytes(filter_grad_got.at[pl.ds(0, (groups - 1) * parts)], relay_sem.at[1, i])
        for r in range(rows):
            filter_grad_ref[own, r * LANES:(r + 1) * LANES] = filter_grad_got[own, r, :]

    for i in range(count):
        wait_bytes(send_f.at[i, pl.ds(0, parts - 1)], f_sem.at[0, i])
        wait_bytes(send_gx.at[i, pl.ds(0, devices - 1)], gx_sem.at[0, i])
        wait_bytes(send_filter_grad.at[i, pl.ds(0, parts - 1)], filter_grad_sem.at[0, i])
        wait_bytes(send_through.at[i, pl.ds(0, devices - 1)], through_sem.at[0, i])
        wait_bytes(filter_grad_got.at[pl.ds(0, (groups - 1) * parts)], relay_sem.at[0, i])


def fused_body(groups, parts, inputs, cotangent, filters, skip_gain):
    channels, width = filters.shape
    rows, half = width // LANES, parts * width // LANES
    devices = groups * parts
    count = channels // devices
    outer, phi, inner, back = dft_tables(parts * width)
    outer_high, outer_low = np_split(outer)
    tables = (
        np.concatenate([outer_high, outer_low], axis=1),
        np.concatenate([outer_high, outer_low, outer_high], axis=1),
        phi,
        np.stack(np_split(inner)),
        np.stack(np_split(inner.T)),
        np.stack(np_split(back)),
    )
    tables = tuple(jnp.asarray(t) for t in tables)
    operands = (inputs, cotangent, filters) + tables + (skip_gain.reshape(1, channels),)
    tile = (rows, LANES)
    return pl.pallas_call(
        functools.partial(kernel, groups, parts, count, half),
        out_shape=(
            jax.ShapeDtypeStruct(cotangent.shape, jnp.bfloat16),
            jax.ShapeDtypeStruct(filters.shape, jnp.float32),
        ),
        in_specs=[pl.BlockSpec(memory_space=pltpu.HBM)] * len(operands),
        out_specs=(pl.BlockSpec(memory_space=pltpu.VMEM),) * 2,
        scratch_shapes=[pltpu.VMEM(t.shape, t.dtype) for t in operands] + [
            pltpu.VMEM((count, devices, 2) + tile, jnp.float32),
            pltpu.VMEM((count, devices) + tile, jnp.float32),
            pltpu.VMEM((count, devices, 2) + tile, jnp.float32),
            pltpu.VMEM((count, parts) + tile, jnp.float32),
            pltpu.VMEM((count, devices) + tile, jnp.float32),
            pltpu.VMEM((count, parts) + tile, jnp.float32),
            pltpu.VMEM((channels,) + tile, jnp.float32),
            pltpu.VMEM((channels,) + tile, jnp.float32),
            pltpu.SemaphoreType.DMA((len(operands),)),
        ] + [pltpu.SemaphoreType.DMA((2, count))] * 5,
        compiler_params=pltpu.CompilerParams(collective_id=0, has_side_effects=True),
    )(*operands)


def solution(mesh):
    groups, parts = mesh.shape["dp"], mesh.shape["ctx"]

    def body(inputs, cotangent, filters, skip_gain):
        if filters.shape[0] % (groups * parts) or inputs.shape[0] != 1:
            return plain_body(inputs, cotangent, filters, skip_gain)
        return fused_body(groups, parts, inputs, cotangent, filters, skip_gain)

    return jax.shard_map(
        body,
        mesh=mesh,
        in_specs=(P("dp", None, "ctx"), P("dp", None, "ctx"), P(None, "ctx"), P()),
        out_specs=(P("dp", None, "ctx"), P(None, "ctx")),
        check_vma=False,
    )
```

```python
import functools
import math

import jax
import jax.numpy as jnp
import ml_dtypes
import numpy as np
from jax import lax
from jax.experimental import pallas as pl
from jax.experimental.pallas import tpu as pltpu
from jax.sharding import PartitionSpec as P

LANES = 128
MESH = pl.DeviceIdType.MESH


def dft_tables(length):
    half = length // LANES
    row = np.arange(half)
    lane = np.arange(LANES)
    theta = 2 * math.pi / (2 * half) * (((row[:, None] + 0.5) * row[None, :]) % (2 * half))
    outer = np.concatenate([np.cos(theta), -np.sin(theta)])
    phi = math.pi / length * ((row[:, None] + 0.5) * lane[None, :])
    phi_table = np.stack([np.cos(phi), -np.sin(phi)])
    psi = 2 * math.pi / LANES * ((lane[:, None] * lane[None, :]) % LANES)
    cos, sin = np.cos(psi), np.sin(psi)
    inner = np.block([[cos, -sin], [sin, cos]])
    back = outer.T / length / math.sqrt(length)
    return outer, phi_table.astype(np.float32), inner, back


def np_split(table):
    high = table.astype(ml_dtypes.bfloat16)
    low = (table - high.astype(np.float64)).astype(ml_dtypes.bfloat16)
    return high, low


def split(values):
    high = values.astype(jnp.bfloat16)
    return high, (values - high.astype(jnp.float32)).astype(jnp.bfloat16)


def dot(left, right):
    return jnp.dot(left, right, preferred_element_type=jnp.float32)


def plain_gradients(grads, inputs, filters):
    batch, channels, length = grads.shape
    half = length // LANES
    outer, phi, inner, back = dft_tables(length)
    outer, inner, back = (t.astype(np.float32) for t in (outer, inner, back))
    product = functools.partial(jnp.matmul, precision=lax.Precision.HIGHEST)

    def forward(values):
        rows = product(outer, values.reshape(values.shape[:-1] + (half, LANES)))
        real, imag = rows[..., :half, :], rows[..., half:, :]
        turned = jnp.concatenate(
            [real * phi[0] - imag * phi[1], real * phi[1] + imag * phi[0]], axis=-1
        )
        spec = product(turned, inner)
        return spec[..., :LANES], spec[..., LANES:]

    def backward(real, imag):
        rows = product(jnp.concatenate([real, imag], axis=-1), inner.T)
        real, imag = rows[..., :LANES], rows[..., LANES:]
        turned = jnp.concatenate(
            [real * phi[0] + imag * phi[1], imag * phi[0] - real * phi[1]], axis=-2
        )
        out = product(back, turned)
        return out.reshape(out.shape[:-2] + (length,))

    def conj_product(first, second):
        return (
            first[0] * second[0] + first[1] * second[1],
            first[0] * second[1] - first[1] * second[0],
        )

    grad_spec = forward(grads)
    through = backward(*conj_product(forward(filters), grad_spec))
    real, imag = conj_product(forward(inputs), grad_spec)
    return through, backward(real.sum(0), imag.sum(0))


def plain_body(inputs, cotangent, filters, skip_gain):
    def gather(values):
        return lax.all_to_all(values, "ctx", 0, 1, tiled=True)

    grad_rows = cotangent[0].astype(jnp.float32)
    grads, rows = gather(grad_rows), gather(inputs[0].astype(jnp.float32))
    through, filter_grad = plain_gradients(grads[None], rows[None], gather(filters))
    filter_grad = lax.psum(filter_grad, "dp")
    through = lax.all_to_all(through[0], "ctx", 1, 0, tiled=True)
    filter_grad = lax.all_to_all(filter_grad, "ctx", 1, 0, tiled=True)
    return (through + skip_gain[:, None] * grad_rows).astype(jnp.bfloat16)[None], filter_grad


def kernel(
    groups, parts, count, half,
    x_hbm, g_hbm, f_hbm, outer_hbm, outer3_hbm, phi_hbm, inner_hbm, inner_t_hbm, back_hbm,
    skip_hbm,
    input_grad_ref, filter_grad_ref,
    x_ref, g_ref, f_ref, outer_ref, outer3_ref, phi_ref, inner_ref, inner_t_ref, back_ref,
    skip_ref,
    send_gx, send_f, recv_gx, recv_f, send_through, send_filter_grad,
    through_got, filter_grad_got,
    load_sem, gx_sem, f_sem, through_sem, filter_grad_sem, relay_sem,
):
    devices = groups * parts
    rows = x_ref.shape[2] // LANES
    group, part = lax.axis_index("dp"), lax.axis_index("ctx")
    me = group * parts + part

    loads = [
        pltpu.make_async_copy(source, target, load_sem.at[n])
        for n, (source, target) in enumerate(
            [
                (g_hbm, g_ref), (x_hbm, x_ref), (f_hbm, f_ref),
                (outer_hbm, outer_ref), (outer3_hbm, outer3_ref), (phi_hbm, phi_ref),
                (inner_hbm, inner_ref), (inner_t_hbm, inner_t_ref), (back_hbm, back_ref),
                (skip_hbm, skip_ref),
            ]
        )
    ]
    for load in loads:
        load.start()

    def after(position, step, size):
        moved = position + step
        return jnp.where(moved >= size, moved - size, moved)

    others = [after(part, step, parts) for step in range(parts)]

    def each_other(act):
        for turn in range(parts):
            for lead in range(groups):
                step = (turn + lead * parts // groups) % parts
                if lead or step:
                    act(after(group, lead, groups), others[step])

    barrier = pltpu.get_barrier_semaphore()
    each_other(
        lambda to_group, to_part: pl.semaphore_signal(
            barrier, inc=1, device_id=(to_group, to_part), device_id_type=MESH
        )
    )

    def remote(source, target, sems, i, to_group, to_part):
        pltpu.make_async_remote_copy(
            src_ref=source,
            dst_ref=target,
            send_sem=sems.at[0, i],
            recv_sem=sems.at[1, i],
            device_id=(to_group, to_part),
            device_id_type=MESH,
        ).start()

    def wait_bytes(held, sem):
        pltpu.make_async_copy(held, held, sem).wait()

    def pack(i):
        own = slice(i * devices, (i + 1) * devices)
        for r in range(rows):
            lanes = slice(r * LANES, (r + 1) * LANES)
            send_gx[i, :, 0, r, :] = g_ref[0, own, lanes].astype(jnp.float32)
            send_gx[i, :, 1, r, :] = x_ref[0, own, lanes].astype(jnp.float32)
            send_f[i, :, r, :] = f_ref[own, lanes]

    def send_rows(i):
        for other in others[1:]:
            remote(
                send_f.at[i, group * parts + other], recv_f.at[i, part], f_sem, i, group, other
            )

        each_other(
            lambda to_group, to_part: remote(
                send_gx.at[i, to_group * parts + to_part], recv_gx.at[i, me],
                gx_sem, i, to_group, to_part,
            )
        )
        recv_gx[i, me] = send_gx[i, me]
        recv_f[i, part] = send_f[i, me]

    for load in loads[:3]:
        load.wait()
    pack(0)
    pl.semaphore_wait(barrier, devices - 1)
    send_rows(0)
    for i in range(1, count):
        pack(i)
        send_rows(i)
    for load in loads[3:]:
        load.wait()

    def product3(left, right):
        (left_high, left_low), (right_high, right_low) = left, right
        return (
            dot(left_high, right_high) + dot(left_low, right_high) + dot(left_high, right_low)
        )

    def turn(real, imag, sine):
        cosine = phi_ref[0]
        return real * cosine - imag * sine, real * sine + imag * cosine

    for i in range(count):
        wait_bytes(recv_f.at[i, pl.ds(0, parts - 1)], f_sem.at[1, i])
        wait_bytes(recv_gx.at[i, pl.ds(0, devices - 1)], gx_sem.at[1, i])

        def signal(kind, b):
            return recv_gx[i, b * parts:(b + 1) * parts, kind].reshape(half, LANES).astype(jnp.bfloat16)

        exact = jnp.concatenate(
            [signal(0, b) for b in range(groups)] + [signal(1, b) for b in range(groups)], axis=1
        )
        def forward(stepped):
            blocks = [stepped[:, k:k + LANES] for k in range(0, stepped.shape[1], LANES)]
            turned = [
                jnp.concatenate(turn(block[:half], block[half:], phi_ref[1]), axis=1)
                for block in blocks
            ]
            return pieces(jnp.concatenate(turned, axis=0), inner_ref)

        def pieces(values, table_ref):
            out = product3(split(values), (table_ref[0], table_ref[1]))
            blocks = [out[k:k + half] for k in range(0, out.shape[0], half)]
            return [(block[:, :LANES], block[:, LANES:]) for block in blocks]

        def backward(specs):
            values = jnp.concatenate([jnp.concatenate(pair, axis=1) for pair in specs], axis=0)
            turned = [
                jnp.concatenate(turn(real, imag, -phi_ref[1]), axis=0)
                for real, imag in pieces(values, inner_t_ref)
            ]
            out = product3((back_ref[0], back_ref[1]), split(jnp.concatenate(turned, axis=1)))
            blocks = [out[:, k:k + LANES] for k in range(0, out.shape[1], LANES)]
            return [block.reshape(parts, rows, LANES) for block in blocks]

        def conj_product(first, second):
            return (
                first[0] * second[0] + first[1] * second[1],
                first[0] * second[1] - first[1] * second[0],
            )

        exact = jnp.concatenate(
            [signal(0, b) for b in range(groups)] + [signal(1, b) for b in range(groups)], axis=1
        )
        specs = forward(dot(outer_ref[...], jnp.concatenate([exact, exact], axis=0)))
        grad_specs, input_specs = specs[:groups], specs[groups:]
        terms = [conj_product(first, second) for first, second in zip(input_specs, grad_specs)]
        real, imag = zip(*terms)
        send_filter_grad[i] = backward([(sum(real[1:], real[0]), sum(imag[1:], imag[0]))])[0]
        channel = i * devices + me
        for other in others[1:]:
            remote(
                send_filter_grad.at[i, other], filter_grad_got.at[channel],
                filter_grad_sem, i, group, other,
            )
        filter_grad_got[channel] = send_filter_grad[i, part]

        high, low = split(recv_f[i].reshape(half, LANES))
        filter_part = dot(outer3_ref[...], jnp.concatenate([high, high, low], axis=0))
        filter_spec = forward(filter_part)[0]
        for b, tiles in enumerate(backward([conj_product(filter_spec, g) for g in grad_specs])):
            send_through[i, b * parts:(b + 1) * parts] = tiles
        each_other(
            lambda to_group, to_part: remote(
                send_through.at[i, to_group * parts + to_part], through_got.at[channel],
                through_sem, i, to_group, to_part,
            )
        )
        through_got[channel] = send_through[i, me]

    def held_by(i, b):
        return filter_grad_got.at[pl.ds(i * devices + b * parts, parts)]

    for i in range(count):
        wait_bytes(
            filter_grad_got.at[pl.ds(i * devices, parts - 1)], filter_grad_sem.at[1, i]
        )
        for lead in range(1, groups):
            remote(
                held_by(i, group), held_by(i, group), relay_sem, i, after(group, lead, groups), part
            )

    size = skip_ref.shape[1]
    square = (size, size)
    on_diagonal = (
        lax.broadcasted_iota(jnp.int32, square, 0) == lax.broadcasted_iota(jnp.int32, square, 1)
    )
    skip = jnp.sum(jnp.where(on_diagonal, skip_ref[...], 0.0), axis=1, keepdims=True)
    for i in range(count):
        own = slice(i * devices, (i + 1) * devices)
        wait_bytes(send_through.at[i, pl.ds(0, devices - 1)], through_sem.at[1, i])
        for r in range(rows):
            lanes = slice(r * LANES, (r + 1) * LANES)
            skipped = skip[own] * g_ref[0, own, lanes].astype(jnp.float32)
            input_grad_ref[0, own, lanes] = (through_got[own, r, :] + skipped).astype(jnp.bfloat16)
        wait_bytes(filter_grad_got.at[pl.ds(0, (groups - 1) * parts)], relay_sem.at[1, i])
        for r in range(rows):
            filter_grad_ref[own, r * LANES:(r + 1) * LANES] = filter_grad_got[own, r, :]

    for i in range(count):
        wait_bytes(send_f.at[i, pl.ds(0, parts - 1)], f_sem.at[0, i])
        wait_bytes(send_gx.at[i, pl.ds(0, devices - 1)], gx_sem.at[0, i])
        wait_bytes(send_filter_grad.at[i, pl.ds(0, parts - 1)], filter_grad_sem.at[0, i])
        wait_bytes(send_through.at[i, pl.ds(0, devices - 1)], through_sem.at[0, i])
        wait_bytes(filter_grad_got.at[pl.ds(0, (groups - 1) * parts)], relay_sem.at[0, i])


def fused_body(groups, parts, inputs, cotangent, filters, skip_gain):
    channels, width = filters.shape
    rows, half = width // LANES, parts * width // LANES
    devices = groups * parts
    count = channels // devices
    outer, phi, inner, back = dft_tables(parts * width)
    outer_high, outer_low = np_split(outer)
    tables = (
        np.concatenate([outer_high, outer_low], axis=1),
        np.concatenate([outer_high, outer_low, outer_high], axis=1),
        phi,
        np.stack(np_split(inner)),
        np.stack(np_split(inner.T)),
        np.stack(np_split(back)),
    )
    tables = tuple(jnp.asarray(t) for t in tables)
    operands = (inputs, cotangent, filters) + tables + (skip_gain.reshape(1, channels),)
    tile = (rows, LANES)
    return pl.pallas_call(
        functools.partial(kernel, groups, parts, count, half),
        out_shape=(
            jax.ShapeDtypeStruct(cotangent.shape, jnp.bfloat16),
            jax.ShapeDtypeStruct(filters.shape, jnp.float32),
        ),
        in_specs=[pl.BlockSpec(memory_space=pltpu.HBM)] * len(operands),
        out_specs=(pl.BlockSpec(memory_space=pltpu.VMEM),) * 2,
        scratch_shapes=[pltpu.VMEM(t.shape, t.dtype) for t in operands] + [
            pltpu.VMEM((count, devices, 2) + tile, jnp.float32),
            pltpu.VMEM((count, devices) + tile, jnp.float32),
            pltpu.VMEM((count, devices, 2) + tile, jnp.float32),
            pltpu.VMEM((count, parts) + tile, jnp.float32),
            pltpu.VMEM((count, devices) + tile, jnp.float32),
            pltpu.VMEM((count, parts) + tile, jnp.float32),
            pltpu.VMEM((channels,) + tile, jnp.float32),
            pltpu.VMEM((channels,) + tile, jnp.float32),
            pltpu.SemaphoreType.DMA((len(operands),)),
        ] + [pltpu.SemaphoreType.DMA((2, count))] * 5,
        compiler_params=pltpu.CompilerParams(collective_id=0, has_side_effects=True),
    )(*operands)


def solution(mesh):
    groups, parts = mesh.shape["dp"], mesh.shape["ctx"]

    def body(inputs, cotangent, filters, skip_gain):
        if filters.shape[0] % (groups * parts) or inputs.shape[0] != 1:
            return plain_body(inputs, cotangent, filters, skip_gain)
        return fused_body(groups, parts, inputs, cotangent, filters, skip_gain)

    return jax.shard_map(
        body,
        mesh=mesh,
        in_specs=(P("dp", None, "ctx"), P("dp", None, "ctx"), P(None, "ctx"), P()),
        out_specs=(P("dp", None, "ctx"), P(None, "ctx")),
        check_vma=False,
    )
```
